128 devices in a mesh: seq: 16 (over x, z_hi, core), fsdp: 4 (over y), dp: 2 (over z_lo).
Axes of the slice: x: 4, y: 4, z: 4 (z_hi: 2, z_lo: 2; z = z_hi * 2 + z_lo), core: 2. Of those that a mesh axis runs over, the one named last changes fastest.
Arguments:
- frames: bfloat16 [8, 6144, 1024], P(('fsdp', 'dp'), 'seq'), may hold values from -8 to 8
- utterance_valid_length: int32 [8], P(('fsdp', 'dp')), may hold values from 5376 to 6144, as said below
- utterance_span_frames: int32 [8], P(('fsdp', 'dp')), may hold values from 32 to 64, as said below
- upsampler_inproj: bfloat16 [1024, 3072], P('fsdp'), may hold values from -0.125 to 0.125
- upsampler_projection: bfloat16 [1024, 1024], P('fsdp'), may hold values from -0.1875 to 0.1875
- transformer_inproj: bfloat16 [1024, 3072], P('fsdp'), may hold values from -0.125 to 0.125
- transformer_projection: bfloat16 [1024, 1024], P('fsdp'), may hold values from -0.1875 to 0.1875
- cotangent: bfloat16 [8, 6144, 1024], P(('fsdp', 'dp'), 'seq'), may hold values from -6 to 6
Outputs:
- result: bfloat16 [8, 6144, 1024], P(('fsdp', 'dp'), 'seq')
- frame_input_gradient: bfloat16 [8, 6144, 1024], P(('fsdp', 'dp'), 'seq')
- upsampler_inproj_gradient: float32 [1024, 3072], P('fsdp')
- upsampler_projection_gradient: float32 [1024, 1024], P('fsdp')
- transformer_inproj_gradient: float32 [1024, 3072], P('fsdp')
- transformer_projection_gradient: float32 [1024, 1024], P('fsdp')
The draws below stay inside these ranges and needn't reach their ends.
Inputs may be any that keep to these rules, and one draw needn't show every extreme that they name: Frames 0 to utterance_valid_length - 1 of each utterance are valid; some utterance has all 6144 frames valid. `utterance_span_frames`: some utterance uses spans of exactly 64 frames.
All inputs are finite; a program needn't handle non-finite values.
Results may differ from the reference program's by a relative error of at most 0.029.
Values may be sent and summed in bfloat16 or wider, within the bound.
A program may use at most 192 MiB of HBM per device.

```python
import jax
import jax.numpy as jnp
from jax import lax

MODEL_WIDTH = 1024
HEADS = 16
CMAX = 64
FRAMES_PER_SHARD = 384
UTTERANCE_FRAMES = 6144
UTTS = 8
N_SEQ = 16


def draw_frames(key, part):
    key = jax.random.fold_in(key, 3)
    sub_keys = jax.random.split(key, 3)
    frame_shape = (UTTS, UTTERANCE_FRAMES, MODEL_WIDTH)
    return jnp.clip(jax.random.normal(sub_keys[2], frame_shape), -6.0, 6.0).astype(jnp.bfloat16)


def draw_upsampler_inproj(key, part):
    key = jax.random.fold_in(key, 5)
    return (jnp.clip(jax.random.normal(key, (MODEL_WIDTH, 3 * MODEL_WIDTH)), -4.0, 4.0) * MODEL_WIDTH ** (-0.5)).astype(jnp.bfloat16)


def draw_transformer_inproj(key, part):
    key = jax.random.fold_in(key, 7)
    return (jnp.clip(jax.random.normal(key, (MODEL_WIDTH, 3 * MODEL_WIDTH)), -4.0, 4.0) * MODEL_WIDTH ** (-0.5)).astype(jnp.bfloat16)


def draw_utterance_valid_length(key, part):
    key = jax.random.fold_in(key, 11)
    first_key, second_key = jax.random.split(key)
    lengths = jax.random.randint(first_key, (UTTS,), UTTERANCE_FRAMES - 2 * FRAMES_PER_SHARD, UTTERANCE_FRAMES + 1)
    chosen = jax.random.randint(second_key, (), 0, UTTS)
    return jnp.where(jnp.arange(UTTS) == chosen, UTTERANCE_FRAMES, lengths).astype(jnp.int32)


def draw_utterance_span_frames(key, part):
    key = jax.random.fold_in(key, 13)
    first_key, second_key = jax.random.split(key)
    sizes_drawn = jax.random.randint(first_key, (UTTS,), CMAX // 2, CMAX + 1)
    chosen = jax.random.randint(second_key, (), 0, UTTS)
    return jnp.where(jnp.arange(UTTS) == chosen, CMAX, sizes_drawn).astype(jnp.int32)


def level_of(stream_key, extent, pieces, least, top_value):
    level = 1.0
    for position, parts in pieces:
        heights = jax.random.uniform(jax.random.fold_in(jax.random.fold_in(stream_key, 6), position), (parts,), jnp.float32, least / len(pieces), top_value / len(pieces))
        level = level * jnp.repeat(jnp.exp(heights), extent[position] // parts).reshape((-1,) + (1,) * (len(extent) - 1 - position))
    return level


def bell_draw(rng, shape, scale, bound, cuts=(), kind=jnp.bfloat16):
    gain = level_of(rng, shape, cuts, -0.22, 0.18) if cuts else 1.0
    values = jax.random.normal(rng, shape, jnp.float32) * scale * gain
    return jnp.minimum(jnp.maximum(values, -bound), bound).astype(kind)


def setup_inputs(seed: int = 0) -> dict:
    arg_keys = jax.random.split(jax.random.key(seed), 9)
    frames = draw_frames(jax.random.fold_in(arg_keys[8], 71), 0)
    utterance_valid_length = draw_utterance_valid_length(jax.random.fold_in(arg_keys[8], 71), 0)
    utterance_span_frames = draw_utterance_span_frames(jax.random.fold_in(arg_keys[8], 71), 0)
    upsampler_inproj = draw_upsampler_inproj(jax.random.fold_in(arg_keys[8], 71), 0)
    upsampler_projection = bell_draw(arg_keys[4], (MODEL_WIDTH, MODEL_WIDTH), MODEL_WIDTH ** -0.5, 0.1875, ((0, 4),))
    transformer_inproj = draw_transformer_inproj(jax.random.fold_in(arg_keys[8], 71), 0)
    transformer_projection = bell_draw(arg_keys[6], (MODEL_WIDTH, MODEL_WIDTH), MODEL_WIDTH ** -0.5, 0.1875, ((0, 4),))
    cotangent = bell_draw(arg_keys[7], (UTTS, UTTERANCE_FRAMES, MODEL_WIDTH), 1.0, 6.0, ((0, 8), (1, 16)))
    return {"frames": frames, "utterance_valid_length": utterance_valid_length, "utterance_span_frames": utterance_span_frames, "upsampler_inproj": upsampler_inproj, "upsampler_projection": upsampler_projection, "transformer_inproj": transformer_inproj, "transformer_projection": transformer_projection, "cotangent": cotangent}


EPS = 1e-06

def normalize_rows(xfull):
    inverse = lax.rsqrt(lax.optimization_barrier(jnp.mean(xfull * xfull, axis=-1, keepdims=True)) + EPS)
    return (xfull * inverse, inverse)

def norm_backward(xfull, inverse, d_normed):
    row_inner = lax.optimization_barrier(jnp.mean(d_normed * xfull, axis=-1, keepdims=True))
    return inverse * d_normed - xfull * (inverse * inverse * inverse) * row_inner

def span_window_mask(query_positions, key_positions, span_length, frame_length, behind, ahead):
    span_gap = key_positions[None, :] // span_length - query_positions[:, None] // span_length
    live_keys = (key_positions >= 0) & (key_positions < frame_length)
    return (span_gap >= -behind) & (span_gap <= ahead) & live_keys[None, :]

def attend_forward(query, keys, values, allowed, active_query):
    row_total, hidden_width = query.shape
    key_count = keys.shape[0]
    head_dim = hidden_width // HEADS
    query_heads = query.reshape(row_total, HEADS, head_dim).astype(jnp.float32)
    key_heads = keys.reshape(key_count, HEADS, head_dim).astype(jnp.float32)
    value_heads = values.reshape(key_count, HEADS, head_dim).astype(jnp.float32)
    scores = jnp.einsum('rhd,ehd->hre', query_heads, key_heads) * head_dim ** (-0.5)
    scores = jnp.where(allowed[None], scores, -1e+30)
    row_max = lax.optimization_barrier(jnp.max(scores, axis=-1, keepdims=True))
    exp_terms = jnp.exp(scores - row_max)
    attn_prob = exp_terms / lax.optimization_barrier(jnp.sum(exp_terms, axis=-1, keepdims=True))
    low_prob = attn_prob.astype(jnp.bfloat16)
    mixed = jnp.einsum('hre,ehd->rhd', low_prob.astype(jnp.float32), value_heads)
    mixed = mixed * active_query[:, None, None]
    return (mixed.reshape(row_total, hidden_width).astype(jnp.bfloat16), attn_prob, low_prob)

def attend_backward(query, keys, values, attn_prob, low_prob, d_mixed):
    row_total, hidden_width = query.shape
    key_count = keys.shape[0]
    head_dim = hidden_width // HEADS
    query_heads = query.reshape(row_total, HEADS, head_dim).astype(jnp.float32)
    key_heads = keys.reshape(key_count, HEADS, head_dim).astype(jnp.float32)
    value_heads = values.reshape(key_count, HEADS, head_dim).astype(jnp.float32)
    d_heads = d_mixed.reshape(row_total, HEADS, head_dim).astype(jnp.float32)
    d_prob = jnp.einsum('rhd,ehd->hre', d_heads, value_heads)
    row_inner = lax.optimization_barrier(jnp.sum(attn_prob * d_prob, axis=-1, keepdims=True))
    d_score = (attn_prob * (d_prob - row_inner) * head_dim ** (-0.5)).astype(jnp.bfloat16)
    d_query = jnp.einsum('hre,ehd->rhd', d_score.astype(jnp.float32), key_heads)
    d_key = jnp.einsum('hre,rhd->ehd', d_score.astype(jnp.float32), query_heads)
    d_value = jnp.einsum('hre,rhd->ehd', low_prob.astype(jnp.float32), d_heads)
    return (d_query.reshape(row_total, hidden_width), d_key.reshape(key_count, hidden_width), d_value.reshape(key_count, hidden_width))

def received_from_previous(blocks):
    return jnp.concatenate([jnp.zeros_like(blocks[:1]), blocks[:-1]], axis=0)

def received_from_next(blocks):
    return jnp.concatenate([blocks[1:], jnp.zeros_like(blocks[:1])], axis=0)

def block_partials(left, right):
    terms = jnp.einsum('nrd,nre->nde', left.astype(jnp.float32), right.astype(jnp.float32))
    return lax.optimization_barrier(jnp.sum(terms.astype(jnp.bfloat16).astype(jnp.float32), axis=0))

def compute_attention(block_args):
    return attend_forward(block_args[0], block_args[1], block_args[2], block_args[3], block_args[4])

def compute_backward(block_args):
    return attend_backward(block_args[0], block_args[1], block_args[2], block_args[3], block_args[4], block_args[5])

def reshape_into_blocks(array):
    return array.reshape(N_SEQ, FRAMES_PER_SHARD, array.shape[-1])

def utterance_index(packed_output, layer_weights):
    frame_rows, frame_length, span_length, gradient_row_block = packed_output
    upsampler_inproj_weight, upsampler_projection_weight, transformer_inproj_weight, transformer_projection_weight = layer_weights
    rim_ahead = 2 * CMAX
    previous_border = 3 * CMAX
    block_first = jnp.arange(N_SEQ, dtype=jnp.int32) * FRAMES_PER_SHARD
    local_positions = block_first[:, None] + jnp.arange(FRAMES_PER_SHARD, dtype=jnp.int32)[None, :]
    ahead_pos = block_first[:, None] + jnp.arange(FRAMES_PER_SHARD + rim_ahead, dtype=jnp.int32)[None, :]
    previous_positions = block_first[:, None] - previous_border + jnp.arange(previous_border + FRAMES_PER_SHARD, dtype=jnp.int32)[None, :]
    active_query = (local_positions < frame_length).astype(jnp.float32)
    allowed_up = jax.vmap(lambda query_positions, key_positions: span_window_mask(query_positions, key_positions, span_length, frame_length, 0, 1))(local_positions, ahead_pos)
    transformer_allowed = jax.vmap(lambda query_positions, key_positions: span_window_mask(query_positions, key_positions, span_length, frame_length, 2, 0))(local_positions, previous_positions)
    active_flattened = active_query.reshape(UTTERANCE_FRAMES, 1)
    xf_up = frame_rows.astype(jnp.float32)
    nf_up, inv_up = normalize_rows(xf_up)
    normed_up = nf_up.astype(jnp.bfloat16)
    act_up = jnp.dot(normed_up, upsampler_inproj_weight, preferred_element_type=jnp.float32).astype(jnp.bfloat16)
    query_up = reshape_into_blocks(act_up[:, :MODEL_WIDTH])
    key_up = reshape_into_blocks(act_up[:, MODEL_WIDTH:2 * MODEL_WIDTH])
    value_up = reshape_into_blocks(act_up[:, 2 * MODEL_WIDTH:])
    keys_up = jnp.concatenate([key_up, received_from_next(key_up[:, :rim_ahead])], axis=1)
    values_up = jnp.concatenate([value_up, received_from_next(value_up[:, :rim_ahead])], axis=1)
    mix_up, prob_up, low_up = lax.map(compute_attention, (query_up, keys_up, values_up, allowed_up, active_query))
    hidden_state = (xf_up + jnp.dot(mix_up.reshape(UTTERANCE_FRAMES, MODEL_WIDTH), upsampler_projection_weight, preferred_element_type=jnp.float32)).astype(jnp.bfloat16)
    transformer_frames = hidden_state.astype(jnp.float32)
    transformer_normed_frames, transformer_inverse_norm = normalize_rows(transformer_frames)
    transformer_normed = transformer_normed_frames.astype(jnp.bfloat16)
    transformer_activation = jnp.dot(transformer_normed, transformer_inproj_weight, preferred_element_type=jnp.float32).astype(jnp.bfloat16)
    transformer_query = reshape_into_blocks(transformer_activation[:, :MODEL_WIDTH])
    transformer_key = reshape_into_blocks(transformer_activation[:, MODEL_WIDTH:2 * MODEL_WIDTH])
    transformer_value = reshape_into_blocks(transformer_activation[:, 2 * MODEL_WIDTH:])
    transformer_keys = jnp.concatenate([received_from_previous(transformer_key[:, FRAMES_PER_SHARD - previous_border:]), transformer_key], axis=1)
    transformer_values = jnp.concatenate([received_from_previous(transformer_value[:, FRAMES_PER_SHARD - previous_border:]), transformer_value], axis=1)
    transformer_mixed, transformer_probability, transformer_log_prob = lax.map(compute_attention, (transformer_query, transformer_keys, transformer_values, transformer_allowed, active_query))
    result = (transformer_frames + jnp.dot(transformer_mixed.reshape(UTTERANCE_FRAMES, MODEL_WIDTH), transformer_projection_weight, preferred_element_type=jnp.float32)).astype(jnp.bfloat16)
    transformer_mixed_gradient = (jnp.dot(gradient_row_block, transformer_projection_weight.T, preferred_element_type=jnp.float32) * active_flattened).astype(jnp.bfloat16)
    transformer_projection_partial = block_partials(transformer_mixed, reshape_into_blocks(gradient_row_block))
    transformer_query_gradient, transformer_key_gradient, transformer_value_gradient = lax.map(compute_backward, (transformer_query, transformer_keys, transformer_values, transformer_probability, transformer_log_prob, reshape_into_blocks(transformer_mixed_gradient)))
    local_key_gradient = transformer_key_gradient[:, previous_border:].at[:, FRAMES_PER_SHARD - previous_border:].add(received_from_next(transformer_key_gradient[:, :previous_border]))
    local_value_gradient = transformer_value_gradient[:, previous_border:].at[:, FRAMES_PER_SHARD - previous_border:].add(received_from_next(transformer_value_gradient[:, :previous_border]))
    transformer_activation_gradient = jnp.concatenate([transformer_query_gradient, local_key_gradient, local_value_gradient], axis=2).astype(jnp.bfloat16)
    transformer_inproj_partial = block_partials(reshape_into_blocks(transformer_normed), transformer_activation_gradient)
    transformer_normed_gradient = jnp.dot(transformer_activation_gradient.reshape(UTTERANCE_FRAMES, 3 * MODEL_WIDTH), transformer_inproj_weight.T, preferred_element_type=jnp.float32)
    hidden_gradient = (gradient_row_block.astype(jnp.float32) + norm_backward(transformer_frames, transformer_inverse_norm, transformer_normed_gradient)).astype(jnp.bfloat16)
    d_mix_up = (jnp.dot(hidden_gradient, upsampler_projection_weight.T, preferred_element_type=jnp.float32) * active_flattened).astype(jnp.bfloat16)
    upsampler_projection_partial = block_partials(mix_up, reshape_into_blocks(hidden_gradient))
    dq_up, dk_up, dv_up = lax.map(compute_backward, (query_up, keys_up, values_up, prob_up, low_up, reshape_into_blocks(d_mix_up)))
    dk_mine = dk_up[:, :FRAMES_PER_SHARD].at[:, :rim_ahead].add(received_from_previous(dk_up[:, FRAMES_PER_SHARD:]))
    dv_mine = dv_up[:, :FRAMES_PER_SHARD].at[:, :rim_ahead].add(received_from_previous(dv_up[:, FRAMES_PER_SHARD:]))
    dact_up = jnp.concatenate([dq_up, dk_mine, dv_mine], axis=2).astype(jnp.bfloat16)
    upsampler_inproj_partial = block_partials(reshape_into_blocks(normed_up), dact_up)
    dn_up = jnp.dot(dact_up.reshape(UTTERANCE_FRAMES, 3 * MODEL_WIDTH), upsampler_inproj_weight.T, preferred_element_type=jnp.float32)
    frame_input_gradient = (hidden_gradient.astype(jnp.float32) + norm_backward(xf_up, inv_up, dn_up)).astype(jnp.bfloat16)
    return (result, frame_input_gradient, upsampler_inproj_partial, upsampler_projection_partial, transformer_inproj_partial, transformer_projection_partial)

def reference(frames, utterance_valid_length, utterance_span_frames, upsampler_inproj, upsampler_projection, transformer_inproj, transformer_projection, cotangent):
    layer_weights = (upsampler_inproj, upsampler_projection, transformer_inproj, transformer_projection)
    result, frame_input_gradient, upsampler_inproj_total, upsampler_projection_total, transformer_inproj_total, transformer_projection_total = lax.map(lambda packed_output: utterance_index(packed_output, layer_weights), (frames, utterance_valid_length, utterance_span_frames, cotangent))
    softmax_scale = float(UTTS * UTTERANCE_FRAMES) ** (-0.5)
    return (result, frame_input_gradient, lax.optimization_barrier(jnp.sum(upsampler_inproj_total, axis=0)) * softmax_scale, lax.optimization_barrier(jnp.sum(upsampler_projection_total, axis=0)) * softmax_scale, lax.optimization_barrier(jnp.sum(transformer_inproj_total, axis=0)) * softmax_scale, lax.optimization_barrier(jnp.sum(transformer_projection_total, axis=0)) * softmax_scale)
```

```python
import functools
import jax
import jax.numpy as jnp
from jax import lax
from jax.experimental import pallas as pl
from jax.experimental.pallas import tpu as pltpu
from jax.sharding import PartitionSpec as P

LINKS = ("xA", "yB", "zA", "xB", "yA", "zB")
PLANE = ("xA", "zA", "xB", "zB")


class Place:
    def __init__(self):
        seq = lax.axis_index("seq")
        self.y = lax.axis_index("fsdp")
        self.zl = lax.axis_index("dp")
        self.x = seq // 4
        self.zh = (seq // 2) % 2
        self.c = seq % 2
        self.z = self.zh * 2 + self.zl

    def bit(self, link):
        p = {"x": self.x, "y": self.y, "z": self.z}[link[0]]
        return ((p + 1) // 2) % 2 if link[1] == "A" else p // 2

    def peer(self, link):
        x, y, z, c = self.x, self.y, self.z, self.c
        if link == "core":
            c = 1 - c
        elif link[0] == "x":
            x = 3 - x if link[1] == "B" else x + 1 - 2 * (x % 2)
        elif link[0] == "y":
            y = 3 - y if link[1] == "B" else y + 1 - 2 * (y % 2)
        else:
            z = 3 - z if link[1] == "B" else z + 1 - 2 * (z % 2)
        return {"seq": x * 4 + (z // 2) * 2 + c, "fsdp": y, "dp": z % 2}


def greet(me):
    barrier = pltpu.get_barrier_semaphore()
    for link in LINKS + ("core",):
        pl.semaphore_signal(barrier, inc=1, device_id=me.peer(link), device_id_type=pl.DeviceIdType.MESH)
    pl.semaphore_wait(barrier, 7)


class Sems:
    def __init__(self, send, recv):
        self.send, self.recv, self.n = send, recv, 0

    def copy(self, me, link, src, dst):
        k = self.n
        self.n += 1
        return pltpu.make_async_remote_copy(
            src_ref=src, dst_ref=dst, send_sem=self.send.at[k], recv_sem=self.recv.at[k],
            device_id=me.peer(link), device_id_type=pl.DeviceIdType.MESH)


def rows(block, off, count):
    return pl.ds(pl.multiple_of(block * 256 + off, 16), count)


class Gather:
    def __init__(self, me, sems, shard, full, width, at, order):
        self.me, self.sems, self.shard, self.full, self.order = me, sems, shard, full, order
        self.cols = pl.ds(pl.multiple_of(at, 128), width)
        self.sent = []
        y = me.y
        self.a, self.b = y + 1 - 2 * (y % 2), 3 - y
        self.ab = 3 - self.a
        self.steps = len(order) + 1
        self.span = 16 if len(order) > 2 else 256
        self.off = 0
        if len(order) > 2:
            for k, link in enumerate(order[2:]):
                self.off = self.off + me.bit(link) * (16 << k)
        self.wait_for = []

    def own(self):
        return self.shard.at[pl.ds(pl.multiple_of(self.off + 0, 16), self.span), self.cols]

    def blk(self, block):
        return self.full.at[rows(block, self.off, self.span), self.cols]

    def _go(self, link, pairs):
        made = [self.sems.copy(self.me, link, s, d) for s, d in pairs]
        for m in made:
            m.start()
        self.sent += made
        self.wait_for = made

    def start(self, step):
        me = self.me
        if step < 2:
            link = self.order[step]
            pairs = [(self.own(), self.blk(me.y))]
            if step == 1:
                other = self.a if self.order[0] == "yA" else self.b
                pairs.append((self.blk(other), self.blk(other)))
            self._go(link, pairs)
        elif step < len(self.order):
            self._go(self.order[step], [(self.blk(k), self.blk(k)) for k in (self.a, self.b, self.ab)])
        else:
            self._go("core", [(self.blk(k), self.blk(k)) for k in (self.a, self.b, self.ab)])

    def finish(self, step):
        for m in self.wait_for:
            m.wait_recv()
        if 2 <= step < len(self.order):
            link = self.order[step]
            self.off = self.off - self.me.bit(link) * self.span
            self.span *= 2

    def close(self):
        for m in self.sent:
            m.wait_send()


class Reduce:
    def __init__(self, me, sems, terms, acc, inbox, inbox_core, gat, half, width, at, order, gat_order):
        self.me, self.sems, self.terms, self.acc, self.inbox, self.inbox_core, self.gat = me, sems, terms, acc, inbox, inbox_core, gat
        self.width, self.order, self.gat_order = width, order, gat_order
        self.cols = pl.ds(at, width)
        self.mine = pl.ds(pl.multiple_of(me.c * half + at, 128), width)
        self.his = pl.ds(pl.multiple_of((1 - me.c) * half + at, 128), width)
        self.sent = []
        y = me.y
        a, b = y + 1 - 2 * (y % 2), 3 - y
        self.y, self.a, self.b, self.ab = y, a, b, 3 - a
        self.live = None
        self.off, self.span, self.inbox_at = 0, 256, 0
        self.steps = 1 + len(order) + len(gat_order) + 1

    def _go(self, link, pairs):
        made = [self.sems.copy(self.me, link, s, d) for s, d in pairs]
        for m in made:
            m.start()
        self.sent += made
        self.wait_for = made

    def start(self, step):
        me = self.me
        if step == 0:
            self._go("core", [(self.terms.at[:, self.his], self.inbox_core.at[:, self.cols])])
            return
        if step <= len(self.order):
            link = self.order[step - 1]
            bit = me.bit(link)
            if link[0] == "y":
                y, a, b, ab = self.y, self.a, self.b, self.ab
                if self.live is None:
                    keep, send = ([y, b], [a, ab]) if link[1] == "A" else ([y, a], [b, ab])
                else:
                    keep, send = [y], [a if link[1] == "A" else b]
                self.live = keep
                keep_off = send_off = self.off
            else:
                self.span //= 2
                live = [0, 1, 2, 3] if self.live is None else self.live
                keep = send = live
                keep_off = self.off + bit * self.span
                send_off = self.off + (1 - bit) * self.span
                self.off = keep_off
            pairs, self.adds = [], []
            for k, s in zip(keep, send, strict=True):
                box = pl.ds(self.inbox_at, self.span)
                pairs.append((self.acc.at[rows(s, send_off, self.span), self.cols], self.inbox.at[box, self.cols]))
                self.adds.append((k * 256 + keep_off, self.inbox_at, self.span))
                self.inbox_at += self.span
            self._go(link, pairs)
            return
        j = step - 1 - len(self.order)
        if j < len(self.gat_order):
            here = self.gat.at[pl.ds(pl.multiple_of(self.off, 16), self.span), self.mine]
            self._go(self.gat_order[j], [(here, here)])
            return
        here = self.gat.at[:, self.mine]
        self._go("core", [(here, here)])

    def finish(self, step):
        for m in self.wait_for:
            m.wait_recv()
        if step == 0:
            @pl.loop(0, 1024 // 64)
            def _(i):
                r = pl.ds(pl.multiple_of(i * 64, 64), 64)
                self.acc[r, self.cols] = self.terms[r, self.mine] + self.inbox_core[r, self.cols]
        elif step <= len(self.order):
            for at, box, count in self.adds:
                chunk = min(count, 64)

                @pl.loop(0, count // chunk)
                def _(i):
                    r = pl.ds(pl.multiple_of(at + i * chunk, 16), chunk)
                    q = pl.ds(pl.multiple_of(box + i * chunk, 16), chunk)
                    self.acc[r, self.cols] = self.acc[r, self.cols] + self.inbox[q, self.cols]
            if step == len(self.order):
                self.gat[pl.ds(pl.multiple_of(self.off, 16), self.span), self.mine] = self.acc[
                    rows(self.y, self.off, self.span), self.cols]
        elif step <= len(self.order) + len(self.gat_order):
            link = self.gat_order[step - 1 - len(self.order)]
            self.off = self.off - self.me.bit(link) * self.span
            self.span *= 2

    def close(self):
        for m in self.sent:
            m.wait_send()


def rotated(i):
    return tuple(LINKS[(i + j) % 6] for j in range(6))


def reduce_parts(me, sems, terms, acc, inbox, inbox_core, gat):
    cols = terms.shape[1]
    half = cols // 2
    n, starts = (6, (0, 1, 2, 3, 4, 5)) if cols == 3072 else (4, (0, 1, 3, 4))
    width = half // n
    out = []
    for i in range(n):
        order = rotated(starts[i])
        back = tuple(l for l in reversed(order) if l[0] != "y")
        out.append(Reduce(me, sems, terms, acc, inbox, inbox_core, gat, half, width, i * width, order, back))
    return out


def gather_parts(me, sems, shard, full):
    cols = full.shape[1]
    half = cols // 2
    tiles = half // 128
    plans = []
    planes = [tuple(PLANE[(i + j) % 4] for j in range(4)) for i in range(4)]
    if tiles == 12:
        at = 0
        for i in range(4):
            plans.append((256, at, (("yA", "yB") if i % 2 else ("yB", "yA")) + planes[i]))
            at += 256
        plans.append((256, at, ("yA", "yB")))
        plans.append((256, at + 256, ("yB", "yA")))
    else:
        for i in range(4):
            plans.append((128, i * 128, (("yA", "yB") if i % 2 else ("yB", "yA")) + planes[i]))
    return [Gather(me, sems, shard, full, w, me.c * half + at, order) for w, at, order in plans]


def run_lockstep(parts):
    steps = max(p.steps for p in parts)
    for s in range(steps):
        for p in parts:
            if s < p.steps:
                p.start(s)
        for p in parts:
            if s < p.steps:
                p.finish(s)
    for p in parts:
        p.close()


def gather_kernel(s0, s1, s2, s3, f0, f1, f2, f3, send, recv, local):
    me = Place()
    own = []
    for k, (s, f) in enumerate(((s0, f0), (s1, f1), (s2, f2), (s3, f3))):
        cp = pltpu.make_async_copy(s, f.at[rows(me.y, 0, 256), :], local.at[k])
        cp.start()
        own.append(cp)
    greet(me)
    sems = Sems(send, recv)
    parts = []
    for s, f in ((s0, f0), (s1, f1), (s2, f2), (s3, f3)):
        parts += gather_parts(me, sems, s, f)
    run_lockstep(parts)
    for cp in own:
        cp.wait()


def gather_weights(*shards):
    anyspec = pl.BlockSpec(memory_space=pl.ANY)
    return pl.pallas_call(
        gather_kernel,
        out_shape=[jax.ShapeDtypeStruct((1024, s.shape[1]), s.dtype) for s in shards],
        in_specs=[anyspec] * 4,
        out_specs=[anyspec] * 4,
        scratch_shapes=[pltpu.SemaphoreType.DMA((400,)), pltpu.SemaphoreType.DMA((400,)), pltpu.SemaphoreType.DMA((4,))],
        compiler_params=pltpu.CompilerParams(collective_id=1, has_side_effects=True, vmem_limit_bytes=32 << 20),
        name="gather_weights",
    )(*shards)


def reduce_kernel(scale, n, *refs):
    terms, outs = refs[:n], refs[n:2 * n]
    acc, inbox, core, gat = (refs[2 * n + i * n:3 * n + i * n] for i in range(4))
    send, recv = refs[6 * n:]
    me = Place()
    greet(me)
    sems = Sems(send, recv)
    parts = []
    for k in range(n):
        parts += reduce_parts(me, sems, terms[k], acc[k], inbox[k], core[k], gat[k])
    run_lockstep(parts)
    for k in range(n):
        @pl.loop(0, 16)
        def _(i):
            r = pl.ds(pl.multiple_of(i * 16, 16), 16)
            outs[k][r, :] = gat[k][r, :].astype(jnp.float32) * scale


def reduce_terms(scale, cid, *terms):
    n = len(terms)
    v = pl.BlockSpec(memory_space=pltpu.VMEM)
    bf = jnp.bfloat16
    scratch = [pltpu.VMEM((1024, t.shape[1] // 2), bf) for t in terms]
    scratch += [pltpu.VMEM((1024, t.shape[1] // 2), bf) for t in terms]
    scratch += [pltpu.VMEM((1024, t.shape[1] // 2), bf) for t in terms]
    scratch += [pltpu.VMEM((256, t.shape[1]), bf) for t in terms]
    return pl.pallas_call(
        functools.partial(reduce_kernel, scale, n),
        out_shape=[jax.ShapeDtypeStruct((256, t.shape[1]), jnp.float32) for t in terms],
        in_specs=[v] * n,
        out_specs=[v] * n,
        scratch_shapes=scratch + [pltpu.SemaphoreType.DMA((500,)), pltpu.SemaphoreType.DMA((500,))],
        compiler_params=pltpu.CompilerParams(collective_id=cid, has_side_effects=True, vmem_limit_bytes=60 << 20),
        name="reduce_terms",
    )(*terms)


FAR = -1e30


def heads_apart(block):
    first = lax.broadcasted_iota(jnp.int32, block.shape, 1) < 64
    zero = jnp.zeros_like(block)
    return jnp.concatenate([jnp.where(first, block, zero), jnp.where(first, zero, block)], axis=0)


def heads_together(wide):
    count = wide.shape[1] // 2
    return jnp.concatenate([wide[:64, :count], wide[64:, count:]], axis=0).T


def nt(a, b):
    return lax.dot_general(a, b, (((1,), (1,)), ((), ())), preferred_element_type=jnp.float32)


def tn(a, b):
    return lax.dot_general(a, b, (((0,), (0,)), ((), ())), preferred_element_type=jnp.float32)


def nn(a, b):
    return jnp.dot(a, b, preferred_element_type=jnp.float32)


def window_bias(key_span, query_span, low, high):
    gap = key_span - query_span
    return jnp.where((gap >= low) & (gap <= high), 0.0, FAR).astype(jnp.float32)


def prob_of(keys, queries, bias):
    score = nt(keys, queries) + jnp.concatenate([bias, bias], axis=1)
    terms = jnp.exp(score - jnp.max(score, axis=0, keepdims=True))
    return terms * (1.0 / jnp.sum(terms, axis=0, keepdims=True))


UP_BLOCKS = ((0, 0, 256), (128, 64, 320), (256, 192, 320))
DIT_BLOCKS = ((0, 0, 384), (128, 128, 384), (256, 256, 320))


def up_forward_kernel(q, k, v, kh, vh, qs, ks, live, mix, kx, vx, bias):
    @pl.when(pl.program_id(0) == 0)
    def _():
        for i, (r0, k0, n) in enumerate(UP_BLOCKS):
            bias[i, :n] = window_bias(ks[k0:k0 + n], qs[:, r0:r0 + 128], 0, 1)
    kx[:384], kx[384:] = k[...], kh[...]
    vx[:384], vx[384:] = v[...], vh[...]
    for i, (r0, k0, n) in enumerate(UP_BLOCKS):
        queries = heads_apart(q[r0:r0 + 128] * jnp.bfloat16(0.125))
        p = prob_of(kx[k0:k0 + n], queries, bias[i, :n])
        out = tn(vx[k0:k0 + n], p.astype(jnp.bfloat16))
        mix[r0:r0 + 128] = (heads_together(out) * live[r0:r0 + 128]).astype(jnp.bfloat16)


def up_backward_kernel(q, k, v, kh, vh, dm, qs, ks, dq, dk, dv, dkh, dvh, kx, vx, bias, dkx, dvx):
    @pl.when(pl.program_id(0) == 0)
    def _():
        for i, (r0, k0, n) in enumerate(UP_BLOCKS):
            bias[i, :n] = window_bias(ks[k0:k0 + n], qs[:, r0:r0 + 128], 0, 1)
    kx[:384], kx[384:] = k[...], kh[...]
    vx[:384], vx[384:] = v[...], vh[...]
    dkx[...] = jnp.zeros_like(dkx)
    dvx[...] = jnp.zeros_like(dvx)
    for i, (r0, k0, n) in enumerate(UP_BLOCKS):
        keys, values = kx[k0:k0 + n], vx[k0:k0 + n]
        queries = heads_apart(q[r0:r0 + 128] * jnp.bfloat16(0.125))
        p = prob_of(keys, queries, bias[i, :n])
        backward_block(p, p.astype(jnp.bfloat16), keys, values, queries, heads_apart(dm[r0:r0 + 128]), r0, k0, n, dq, dkx, dvx)
    dk[...], dkh[...] = dkx[:384], dkx[384:].astype(jnp.bfloat16)
    dv[...], dvh[...] = dvx[:384], dvx[384:].astype(jnp.bfloat16)


def backward_block(p, low, keys, values, queries, dout, r0, k0, n, dq, dkx, dvx):
    dp = nt(values, dout)
    ds = (p * (dp - jnp.sum(p * dp, axis=0, keepdims=True))).astype(jnp.bfloat16)
    dvx[k0:k0 + n] += nn(low, dout)
    dkx[k0:k0 + n] += nn(ds, queries)
    dq[r0:r0 + 128] = (heads_together(tn(keys, ds)) * 0.125).astype(jnp.bfloat16)


def dit_kernel(q, k, v, kh, vh, dm, qs, ks, live, mix, dq, dk, dv, dkh, dvh, kx, vx, bias, dkx, dvx):
    @pl.when(pl.program_id(0) == 0)
    def _():
        for i, (r0, k0, n) in enumerate(DIT_BLOCKS):
            bias[i, :n] = window_bias(ks[k0:k0 + n], qs[:, r0:r0 + 128], -2, 0)
    kx[:192], kx[192:] = kh[...], k[...]
    vx[:192], vx[192:] = vh[...], v[...]
    dkx[...] = jnp.zeros_like(dkx)
    dvx[...] = jnp.zeros_like(dvx)
    for i, (r0, k0, n) in enumerate(DIT_BLOCKS):
        keys, values = kx[k0:k0 + n], vx[k0:k0 + n]
        queries = heads_apart(q[r0:r0 + 128] * jnp.bfloat16(0.125))
        p = prob_of(keys, queries, bias[i, :n])
        low = p.astype(jnp.bfloat16)
        mix[r0:r0 + 128] = (heads_together(tn(values, low)) * live[r0:r0 + 128]).astype(jnp.bfloat16)
        backward_block(p, low, keys, values, queries, heads_apart(dm[r0:r0 + 128]), r0, k0, n, dq, dkx, dvx)
    dk[...], dkh[...] = dkx[192:], dkx[:192].astype(jnp.bfloat16)
    dv[...], dvh[...] = dvx[192:], dvx[:192].astype(jnp.bfloat16)


def cols(rows_, first):
    return pl.BlockSpec((rows_, 128), lambda g: (0, first + g))


def whole(shape):
    return pl.BlockSpec(shape, lambda g: (0, 0))


def attention_call(kernel, rim, name, act, halo, dmix, qs, ks, live, with_mix, with_grad):
    bf, f32 = jnp.bfloat16, jnp.float32
    ext = 384 + rim
    ins = [act, act, act, halo, halo]
    specs = [cols(384, 0), cols(384, 8), cols(384, 16), cols(rim, 0), cols(rim, 8)]
    if with_grad:
        ins.append(dmix)
        specs.append(cols(384, 0))
    ins += [qs, ks]
    specs += [whole((1, 384)), whole((ext, 1))]
    outs, ospecs = [], []
    if with_mix:
        ins.append(live)
        specs.append(whole((384, 1)))
        outs.append(jax.ShapeDtypeStruct((384, 1024), bf))
        ospecs.append(cols(384, 0))
    scratch = [pltpu.VMEM((ext, 128), bf), pltpu.VMEM((ext, 128), bf), pltpu.VMEM((3, 384, 128), f32)]
    if with_grad:
        outs += [jax.ShapeDtypeStruct((384, 1024), bf)] + [jax.ShapeDtypeStruct((384, 1024), f32)] * 2 + [jax.ShapeDtypeStruct((rim, 1024), bf)] * 2
        ospecs += [cols(384, 0)] * 3 + [cols(rim, 0)] * 2
        scratch += [pltpu.VMEM((ext, 128), f32), pltpu.VMEM((ext, 128), f32)]
    return pl.pallas_call(
        kernel, grid=(8,), in_specs=specs, out_specs=ospecs, out_shape=outs, scratch_shapes=scratch,
        cost_estimate=pl.CostEstimate(flops=8 << 30, bytes_accessed=10 << 20, transcendentals=0),
        compiler_params=pltpu.CompilerParams(vmem_limit_bytes=40 << 20), name=name,
    )(*ins)


EPS = 1e-06
DEAD = 1 << 20


def normalize_rows(xfull):
    inverse = lax.rsqrt(jnp.mean(xfull * xfull, axis=-1, keepdims=True) + EPS)
    return (xfull * inverse, inverse)


def norm_backward(xfull, inverse, d_normed):
    row_inner = jnp.mean(d_normed * xfull, axis=-1, keepdims=True)
    return inverse * d_normed - xfull * (inverse * inverse * inverse) * row_inner


def shift(block, distance):
    n = lax.axis_size("seq")
    return lax.ppermute(block, "seq", [(i - distance, i) for i in range(n) if 0 <= i - distance < n])


def term(left, right):
    return lax.dot_general(left, right, (((0,), (0,)), ((), ())), preferred_element_type=jnp.float32).astype(jnp.bfloat16)


def local(frames, valid_length, span_frames, w1_shard, p1_shard, w2_shard, p2_shard, cotangent):
    bf, f32 = jnp.bfloat16, jnp.float32
    x0, cot = frames[0], cotangent[0]
    length, span = valid_length[0], span_frames[0]
    first = lax.axis_index("seq") * 384
    here = first + jnp.arange(384, dtype=jnp.int32)
    query_span = (here // span)[None, :]
    live = (here < length).astype(f32)[:, None]

    def key_span(positions):
        alive = (positions >= 0) & (positions < length)
        return jnp.where(alive, positions // span, DEAD)[:, None]

    ahead_span = key_span(first + jnp.arange(512, dtype=jnp.int32))
    behind_span = key_span(first - 192 + jnp.arange(576, dtype=jnp.int32))

    w1, p1, w2, p2 = gather_weights(w1_shard, p1_shard, w2_shard, p2_shard)

    x0f = x0.astype(f32)
    n0f, inv0 = normalize_rows(x0f)
    n0 = n0f.astype(bf)
    act1 = nn(n0, w1).astype(bf)
    halo1 = shift(act1[:128, 1024:], -1)
    (mix1,) = attention_call(up_forward_kernel, 128, "up_forward", act1, halo1, None, query_span, ahead_span, live, True, False)
    hidden = (x0f + nn(mix1, p1)).astype(bf)
    hf = hidden.astype(f32)
    n1f, inv1 = normalize_rows(hf)
    n1 = n1f.astype(bf)
    act2 = nn(n1, w2).astype(bf)
    halo2 = shift(act2[192:, 1024:], 1)
    dmix2 = (nt(cot, p2) * live).astype(bf)
    mix2, dq2, dk2, dv2, dkh2, dvh2 = attention_call(
        dit_kernel, 192, "dit", act2, halo2, dmix2, query_span, behind_span, live, True, True)
    result = (hf + nn(mix2, p2)).astype(bf)
    gp2 = term(mix2, cot)
    back2 = shift(jnp.concatenate([dkh2, dvh2], axis=1), -1).astype(f32)
    late = jnp.pad(back2, ((192, 0), (0, 0)))
    dact2 = jnp.concatenate([dq2, (dk2 + late[:, :1024]).astype(bf), (dv2 + late[:, 1024:]).astype(bf)], axis=1)
    gw2 = term(n1, dact2)
    dhidden = (cot.astype(f32) + norm_backward(hf, inv1, nt(dact2, w2))).astype(bf)
    dmix1 = (nt(dhidden, p1) * live).astype(bf)
    gp1 = term(mix1, dhidden)
    dq1, dk1, dv1, dkh1, dvh1 = attention_call(
        up_backward_kernel, 128, "up_backward", act1, halo1, dmix1, query_span, ahead_span, live, False, True)
    back1 = shift(jnp.concatenate([dkh1, dvh1], axis=1), 1).astype(f32)
    early = jnp.pad(back1, ((0, 256), (0, 0)))
    dact1 = jnp.concatenate([dq1, (dk1 + early[:, :1024]).astype(bf), (dv1 + early[:, 1024:]).astype(bf)], axis=1)
    gw1 = term(n0, dact1)
    dframes = (dhidden.astype(f32) + norm_backward(x0f, inv0, nt(dact1, w1))).astype(bf)
    scale = float(8 * 6144) ** -0.5
    tw1, tp1, tw2, tp2 = reduce_terms(scale, 2, gw1, gp1, gw2, gp2)
    return (result[None], dframes[None], tw1, tp1, tw2, tp2)


def solution(mesh):
    rows3, row, flat = P(("fsdp", "dp"), "seq", None), P("fsdp", None), P(("fsdp", "dp"))
    return jax.shard_map(
        local, mesh=mesh, in_specs=(rows3, flat, flat, row, row, row, row, rows3),
        out_specs=(rows3, rows3, row, row, row, row), check_vma=False)
```

```python
import functools
import heapq
import jax
import jax.numpy as jnp
from jax import lax
from jax.experimental import pallas as pl
from jax.experimental.pallas import tpu as pltpu
from jax.sharding import PartitionSpec as P

LINKS = ("xA", "yB", "zA", "xB", "yA", "zB")
PLANE = ("xA", "zA", "xB", "zB")


class Place:
    def __init__(self):
        seq = lax.axis_index("seq")
        self.seq = seq
        self.y = lax.axis_index("fsdp")
        self.zl = lax.axis_index("dp")
        self.x = seq // 4
        self.zh = (seq // 2) % 2
        self.c = seq % 2
        self.z = self.zh * 2 + self.zl

    def bit(self, link):
        p = {"x": self.x, "y": self.y, "z": self.z}[link[0]]
        return ((p + 1) // 2) % 2 if link[1] == "A" else p // 2

    def peer(self, link):
        x, y, z, c = self.x, self.y, self.z, self.c
        if link == "core":
            c = 1 - c
        elif link in ("next", "previous"):
            pass
        elif link[0] == "x":
            x = 3 - x if link[1] == "B" else x + 1 - 2 * (x % 2)
        elif link[0] == "y":
            y = 3 - y if link[1] == "B" else y + 1 - 2 * (y % 2)
        else:
            z = 3 - z if link[1] == "B" else z + 1 - 2 * (z % 2)
        if link == "next":
            return {"seq": (self.seq + 1) % 16, "fsdp": y, "dp": self.zl}
        if link == "previous":
            return {"seq": (self.seq + 15) % 16, "fsdp": y, "dp": self.zl}
        return {"seq": x * 4 + (z // 2) * 2 + c, "fsdp": y, "dp": z % 2}


def greet(me, *more):
    barrier = pltpu.get_barrier_semaphore()
    for link in LINKS + ("core",) + more:
        pl.semaphore_signal(barrier, inc=1, device_id=me.peer(link), device_id_type=pl.DeviceIdType.MESH)
    pl.semaphore_wait(barrier, 7 + len(more))


class Sems:
    def __init__(self, send, recv):
        self.send, self.recv, self.n = send, recv, 0

    def copy(self, me, link, src, dst):
        k = self.n
        self.n += 1
        return pltpu.make_async_remote_copy(
            src_ref=src, dst_ref=dst, send_sem=self.send.at[k], recv_sem=self.recv.at[k],
            device_id=me.peer(link), device_id_type=pl.DeviceIdType.MESH)


def rows(block, off, count):
    return pl.ds(pl.multiple_of(block * 256 + off, 16), count)


class Gather:
    def __init__(self, me, sems, shard, full, width, at, order):
        self.me, self.sems, self.shard, self.full, self.order = me, sems, shard, full, order
        self.cols = pl.ds(pl.multiple_of(at, 128), width)
        self.width = width
        self.sent = []
        y = me.y
        self.a, self.b = y + 1 - 2 * (y % 2), 3 - y
        self.ab = 3 - self.a
        self.steps = len(order) + 1
        self.span = 16 if len(order) > 2 else 256
        self.off = 0
        if len(order) > 2:
            for k, link in enumerate(order[2:]):
                self.off = self.off + me.bit(link) * (16 << k)
        self.wait_for = []

    def own(self):
        return self.shard.at[pl.ds(pl.multiple_of(self.off + 0, 16), self.span), self.cols]

    def blk(self, block):
        return self.full.at[rows(block, self.off, self.span), self.cols]

    def _go(self, link, pairs):
        made = [self.sems.copy(self.me, link, s, d) for s, d in pairs]
        for m in made:
            m.start()
        self.sent += made
        self.wait_for = made

    def start(self, step):
        me = self.me
        if step < 2:
            link = self.order[step]
            pairs = [(self.own(), self.blk(me.y))]
            if step == 1:
                other = self.a if self.order[0] == "yA" else self.b
                pairs.append((self.blk(other), self.blk(other)))
            self._go(link, pairs)
        elif step < len(self.order):
            self._go(self.order[step], [(self.blk(k), self.blk(k)) for k in (self.a, self.b, self.ab)])
        else:
            self._go("core", [(self.blk(k), self.blk(k)) for k in (self.a, self.b, self.ab)])

    def load(self, step):
        blocks = 1 if step == 0 else 2 if step == 1 else 3
        return (self.order + ("core",))[step], blocks * self.span * self.width * 2, 0.0

    def finish(self, step):
        for m in self.wait_for:
            m.wait_recv()
        if 2 <= step < len(self.order):
            link = self.order[step]
            self.off = self.off - self.me.bit(link) * self.span
            self.span *= 2

    def close(self):
        for m in self.sent:
            m.wait_send()


class Reduce:
    def __init__(self, me, sems, source, acc, inbox, inbox_core, gat, width, at, gat_at, order, ready=None):
        self.me, self.sems, self.source, self.acc, self.inbox, self.inbox_core, self.gat = me, sems, source, acc, inbox, inbox_core, gat
        self.width, self.order, self.ready = width, order, ready
        self.back = tuple(l for l in reversed(order) if l[0] != "y")
        self.cols = pl.ds(at, width)
        self.mine = pl.ds(pl.multiple_of(gat_at, 128), width)
        self.sent = []
        y = me.y
        a, b = y + 1 - 2 * (y % 2), 3 - y
        self.y, self.a, self.b, self.ab = y, a, b, 3 - a
        self.live = None
        self.off, self.span, self.inbox_at = 0, 256, 0
        self.steps = 12
        self.left = 1024

    def _go(self, link, pairs):
        made = [self.sems.copy(self.me, link, s, d) for s, d in pairs]
        for m in made:
            m.start()
        self.sent += made
        self.wait_for = made

    def load(self, step):
        line = 2 * self.width
        if step == 0:
            return "core", 1024 * line, 1024 * line / 1.5e6
        if step <= 6:
            return self.order[step - 1], (512 >> (step - 1)) * line, (512 >> (step - 1)) * line / 1.5e6 + 0.1
        if step <= 10:
            return self.back[step - 7], (16 << (step - 7)) * line, 0.0
        return "core", 256 * line, 0.0

    def start(self, step):
        me = self.me
        if step == 0:
            self._go("core", [(self.source, self.inbox_core.at[:, self.cols])])
        elif step <= 6:
            link = self.order[step - 1]
            bit = me.bit(link)
            if link[0] == "y":
                y, a, b, ab = self.y, self.a, self.b, self.ab
                if self.live is None:
                    keep, send = ([y, b], [a, ab]) if link[1] == "A" else ([y, a], [b, ab])
                else:
                    keep, send = [y], [a if link[1] == "A" else b]
                self.live = keep
                keep_off = send_off = self.off
            else:
                self.span //= 2
                keep = send = [0, 1, 2, 3] if self.live is None else self.live
                keep_off = self.off + bit * self.span
                send_off = self.off + (1 - bit) * self.span
                self.off = keep_off
            pairs, self.adds = [], []
            for k, s in zip(keep, send, strict=True):
                box = pl.ds(self.inbox_at, self.span)
                pairs.append((self.acc.at[rows(s, send_off, self.span), self.cols], self.inbox.at[box, self.cols]))
                self.adds.append((k * 256 + keep_off, self.inbox_at, self.span))
                self.inbox_at += self.span
            self._go(link, pairs)
        elif step <= 10:
            here = self.gat.at[pl.ds(pl.multiple_of(self.off, 16), self.span), self.mine]
            self._go(self.back[step - 7], [(here, here)])
        else:
            here = self.gat.at[:, self.mine]
            self._go("core", [(here, here)])

    def finish(self, step):
        for m in self.wait_for:
            m.wait_recv()
        if step == 0:
            if self.ready is not None:
                self.ready()

            @pl.loop(0, 1024 // 64)
            def _(i):
                r = pl.ds(pl.multiple_of(i * 64, 64), 64)
                self.acc[r, self.cols] = self.acc[r, self.cols] + self.inbox_core[r, self.cols]
        elif step <= 6:
            for at, box, count in self.adds:
                chunk = min(count, 64)

                @pl.loop(0, count // chunk)
                def _(i):
                    r = pl.ds(pl.multiple_of(at + i * chunk, 16), chunk)
                    q = pl.ds(pl.multiple_of(box + i * chunk, 16), chunk)
                    self.acc[r, self.cols] = self.acc[r, self.cols] + self.inbox[q, self.cols]
            if step == 6:
                self.gat[pl.ds(pl.multiple_of(self.off, 16), self.span), self.mine] = self.acc[
                    rows(self.y, self.off, self.span), self.cols]
        elif step <= 10:
            self.off = self.off - self.me.bit(self.back[step - 7]) * self.span
            self.span *= 2

    def close(self):
        for m in self.sent:
            m.wait_send()


class Timeline:
    def __init__(self):
        self.now, self.free, self.queue, self.count, self.parts = 0.0, {}, [], 0, []

    def launch(self, part, step=0):
        if step == 0:
            self.parts.append(part)
        link, size, cost = part.load(step)
        part.start(step)
        begin = max(self.now, self.free.get(link, 0.0))
        end = begin + size / (0.55e6 if link == "core" else 0.046e6)
        self.free[link] = end
        heapq.heappush(self.queue, (end + (1.0 if link == "core" else 2.0), self.count, part, step, cost))
        self.count += 1

    def _one(self):
        end, _, part, step, cost = heapq.heappop(self.queue)
        self.now = max(self.now, end)
        part.finish(step)
        self.now += cost
        if step + 1 < part.steps:
            self.launch(part, step + 1)

    def poll(self):
        while self.queue and self.queue[0][0] <= self.now:
            self._one()

    def work(self, what, time):
        what()
        self.now += time
        self.poll()

    def drain(self):
        while self.queue:
            self._one()
        for part in self.parts:
            part.close()


def rotated(i):
    return tuple(LINKS[(i + j) % 6] for j in range(6))


def reduce_parts(me, sems, terms, acc, inbox, inbox_core, gat, ready):
    columns = terms.shape[1]
    half = columns // 2
    n, starts = (6, (0, 1, 2, 3, 4, 5)) if columns == 3072 else (4, (0, 1, 3, 4))
    width = half // n
    out = []
    for i in range(n):
        source = terms.at[:, pl.ds(pl.multiple_of((1 - me.c) * half + i * width, 128), width)]
        out.append(Reduce(me, sems, source, acc, inbox, inbox_core, gat, width, i * width, me.c * half + i * width,
                          rotated(starts[i]), ready if i == 0 else None))
    return out


def gather_parts(me, sems, shard, full):
    cols = full.shape[1]
    half = cols // 2
    tiles = half // 128
    plans = []
    planes = [tuple(PLANE[(i + j) % 4] for j in range(4)) for i in range(4)]
    if tiles == 12:
        at = 0
        for i in range(4):
            plans.append((256, at, (("yA", "yB") if i % 2 else ("yB", "yA")) + planes[i]))
            at += 256
        plans.append((256, at, ("yA", "yB")))
        plans.append((256, at + 256, ("yB", "yA")))
    else:
        for i in range(4):
            plans.append((128, i * 128, (("yA", "yB") if i % 2 else ("yB", "yA")) + planes[i]))
    return [Gather(me, sems, shard, full, w, me.c * half + at, order) for w, at, order in plans]


def gather_kernel(s0, s1, s2, s3, f0, f1, f2, f3, send, recv, local):
    me = Place()
    own = []
    for k, (s, f) in enumerate(((s0, f0), (s1, f1), (s2, f2), (s3, f3))):
        cp = pltpu.make_async_copy(s, f.at[rows(me.y, 0, 256), :], local.at[k])
        cp.start()
        own.append(cp)
    greet(me)
    sems = Sems(send, recv)
    line = Timeline()
    for s, f in ((s0, f0), (s1, f1), (s2, f2), (s3, f3)):
        for part in gather_parts(me, sems, s, f):
            line.launch(part)
    line.drain()
    for cp in own:
        cp.wait()


def gather_weights(*shards):
    anyspec = pl.BlockSpec(memory_space=pl.ANY)
    return pl.pallas_call(
        gather_kernel,
        out_shape=[jax.ShapeDtypeStruct((1024, s.shape[1]), s.dtype) for s in shards],
        in_specs=[anyspec] * 4,
        out_specs=[anyspec] * 4,
        scratch_shapes=[pltpu.SemaphoreType.DMA((400,)), pltpu.SemaphoreType.DMA((400,)), pltpu.SemaphoreType.DMA((4,))],
        compiler_params=pltpu.CompilerParams(collective_id=1, has_side_effects=True, vmem_limit_bytes=32 << 20),
        name="gather_weights",
    )(*shards)


FAR = -1e30


def heads_apart(block):
    first = lax.broadcasted_iota(jnp.int32, block.shape, 1) < 64
    zero = jnp.zeros_like(block)
    return jnp.concatenate([jnp.where(first, block, zero), jnp.where(first, zero, block)], axis=0)


def heads_together(wide):
    count = wide.shape[1] // 2
    return jnp.concatenate([wide[:64, :count], wide[64:, count:]], axis=0).T


def nt(a, b):
    return lax.dot_general(a, b, (((1,), (1,)), ((), ())), preferred_element_type=jnp.float32)


def tn(a, b):
    return lax.dot_general(a, b, (((0,), (0,)), ((), ())), preferred_element_type=jnp.float32)


def nn(a, b):
    return jnp.dot(a, b, preferred_element_type=jnp.float32)


def window_bias(key_span, query_span, low, high):
    gap = key_span - query_span
    return jnp.where((gap >= low) & (gap <= high), 0.0, FAR).astype(jnp.float32)


def prob_of(keys, queries, bias):
    score = nt(keys, queries) + jnp.concatenate([bias, bias], axis=1)
    terms = jnp.exp(score - jnp.max(score, axis=0, keepdims=True))
    return terms * (1.0 / jnp.sum(terms, axis=0, keepdims=True))


UP_BLOCKS = ((0, 0, 256), (128, 64, 320), (256, 192, 320))
DIT_BLOCKS = ((0, 0, 384), (128, 128, 384), (256, 256, 320))


def up_forward_kernel(q, k, v, kh, vh, qs, ks, live, mix, kx, vx, bias):
    @pl.when(pl.program_id(0) == 0)
    def _():
        for i, (r0, k0, n) in enumerate(UP_BLOCKS):
            bias[i, :n] = window_bias(ks[k0:k0 + n], qs[:, r0:r0 + 128], 0, 1)
    kx[:384], kx[384:] = k[...], kh[...]
    vx[:384], vx[384:] = v[...], vh[...]
    for i, (r0, k0, n) in enumerate(UP_BLOCKS):
        queries = heads_apart(q[r0:r0 + 128] * jnp.bfloat16(0.125))
        p = prob_of(kx[k0:k0 + n], queries, bias[i, :n])
        out = tn(vx[k0:k0 + n], p.astype(jnp.bfloat16))
        mix[r0:r0 + 128] = (heads_together(out) * live[r0:r0 + 128]).astype(jnp.bfloat16)


def backward_block(p, low, keys, values, queries, dout, r0, k0, n, dq, dkx, dvx):
    dp = nt(values, dout)
    ds = (p * (dp - jnp.sum(p * dp, axis=0, keepdims=True))).astype(jnp.bfloat16)
    dvx[k0:k0 + n] += nn(low, dout)
    dkx[k0:k0 + n] += nn(ds, queries)
    dq[r0:r0 + 128] = (heads_together(tn(keys, ds)) * 0.125).astype(jnp.bfloat16)


def dit_kernel(q, k, v, kh, vh, dm, qs, ks, live, mix, dq, dk, dv, dkh, dvh, kx, vx, bias, dkx, dvx):
    @pl.when(pl.program_id(0) == 0)
    def _():
        for i, (r0, k0, n) in enumerate(DIT_BLOCKS):
            bias[i, :n] = window_bias(ks[k0:k0 + n], qs[:, r0:r0 + 128], -2, 0)
    kx[:192], kx[192:] = kh[...], k[...]
    vx[:192], vx[192:] = vh[...], v[...]
    dkx[...] = jnp.zeros_like(dkx)
    dvx[...] = jnp.zeros_like(dvx)
    for i, (r0, k0, n) in enumerate(DIT_BLOCKS):
        keys, values = kx[k0:k0 + n], vx[k0:k0 + n]
        queries = heads_apart(q[r0:r0 + 128] * jnp.bfloat16(0.125))
        p = prob_of(keys, queries, bias[i, :n])
        low = p.astype(jnp.bfloat16)
        mix[r0:r0 + 128] = (heads_together(tn(values, low)) * live[r0:r0 + 128]).astype(jnp.bfloat16)
        backward_block(p, low, keys, values, queries, heads_apart(dm[r0:r0 + 128]), r0, k0, n, dq, dkx, dvx)
    dk[...], dkh[...] = dkx[192:], dkx[:192].astype(jnp.bfloat16)
    dv[...], dvh[...] = dvx[192:], dvx[:192].astype(jnp.bfloat16)


def cols(rows_, first):
    return pl.BlockSpec((rows_, 128), lambda g: (0, first + g))


def whole(shape):
    return pl.BlockSpec(shape, lambda g: (0, 0))


def attention_call(kernel, rim, name, act, halo, dmix, qs, ks, live, with_mix, with_grad):
    bf, f32 = jnp.bfloat16, jnp.float32
    ext = 384 + rim
    ins = [act, act, act, halo, halo]
    specs = [cols(384, 0), cols(384, 8), cols(384, 16), cols(rim, 0), cols(rim, 8)]
    if with_grad:
        ins.append(dmix)
        specs.append(cols(384, 0))
    ins += [qs, ks]
    specs += [whole((1, 384)), whole((ext, 1))]
    outs, ospecs = [], []
    if with_mix:
        ins.append(live)
        specs.append(whole((384, 1)))
        outs.append(jax.ShapeDtypeStruct((384, 1024), bf))
        ospecs.append(cols(384, 0))
    scratch = [pltpu.VMEM((ext, 128), bf), pltpu.VMEM((ext, 128), bf), pltpu.VMEM((3, 384, 128), f32)]
    if with_grad:
        outs += [jax.ShapeDtypeStruct((384, 1024), bf)] + [jax.ShapeDtypeStruct((384, 1024), f32)] * 2 + [jax.ShapeDtypeStruct((rim, 1024), bf)] * 2
        ospecs += [cols(384, 0)] * 3 + [cols(rim, 0)] * 2
        scratch += [pltpu.VMEM((ext, 128), f32), pltpu.VMEM((ext, 128), f32)]
    return pl.pallas_call(
        kernel, grid=(8,), in_specs=specs, out_specs=ospecs, out_shape=outs, scratch_shapes=scratch,
        cost_estimate=pl.CostEstimate(flops=8 << 30, bytes_accessed=10 << 20, transcendentals=0),
        compiler_params=pltpu.CompilerParams(vmem_limit_bytes=40 << 20), name=name,
    )(*ins)

def last_kernel(gp2, gw2, gp1, act, halo, dm, dh, x0, inv, n0t, w1, qs, ks,
                dframes, t1, tp1, t2, tp2,
                acc1, accp1, acc2, accp2, in1, inp1, in2, inp2, co1, cop1, co2, cop2,
                outbox, kx, vx, bias, dkx, dvx, edge, hout, hin, dact, dcat, dn, send, recv, local):
    me = Place()
    bf = jnp.bfloat16
    sems = Sems(send, recv)
    loads = []
    for i, (t, acc) in enumerate(((gp2, accp2), (gw2, acc2), (gp1, accp1))):
        half = t.shape[1] // 2
        cp = pltpu.make_async_copy(t.at[:, pl.ds(pl.multiple_of(me.c * half, 128), half)], acc, local.at[i])
        cp.start()
        loads.append(cp)
    for i, (r0, k0, n) in enumerate(UP_BLOCKS):
        bias[i, :n] = window_bias(ks[k0:k0 + n], qs[:, r0:r0 + 128], 0, 1)
    greet(me, "next", "previous")
    line = Timeline()
    for i, (t, acc, box, core, gat) in enumerate(((gp2, accp2, inp2, cop2, tp2), (gw2, acc2, in2, co2, t2), (gp1, accp1, inp1, cop1, tp1))):
        for part in reduce_parts(me, sems, t, acc, box, core, gat, loads[i].wait):
            line.launch(part)

    flights = {}

    def attend(k):
        @pl.loop(2 * k, 2 * k + 2)
        def _(g):
            at = pl.multiple_of(g * 128, 128)
            q_at, k_at, v_at = pl.ds(at, 128), pl.ds(at + 1024, 128), pl.ds(at + 2048, 128)
            kx[:384], kx[384:] = act[:, k_at], halo[:, q_at]
            vx[:384], vx[384:] = act[:, v_at], halo[:, k_at]
            dkx[...] = jnp.zeros_like(dkx)
            dvx[...] = jnp.zeros_like(dvx)
            for i, (r0, k0, n) in enumerate(UP_BLOCKS):
                keys, values = kx[k0:k0 + n], vx[k0:k0 + n]
                queries = heads_apart(act[r0:r0 + 128, q_at] * jnp.bfloat16(0.125))
                p = prob_of(keys, queries, bias[i, :n])
                dout = heads_apart(dm[r0:r0 + 128, q_at])
                dp = nt(values, dout)
                ds = (p * (dp - jnp.sum(p * dp, axis=0, keepdims=True))).astype(bf)
                dvx[k0:k0 + n] += nn(p.astype(bf), dout)
                dkx[k0:k0 + n] += nn(ds, queries)
                dact[r0:r0 + 128, q_at] = (heads_together(tn(keys, ds)) * 0.125).astype(bf)
            for full, c_at, e_at in ((dkx, k_at, q_at), (dvx, v_at, k_at)):
                edge[:, e_at] = full[:128]
                dact[128:, c_at] = full[128:384].astype(bf)
                hout[:, e_at] = full[384:].astype(bf)

        made = []
        for first in (0, 1024):
            c = pl.ds(first + 256 * k, 256)
            made.append(sems.copy(me, "next", hout.at[:, c], hin.at[:, c]))
        for m in made:
            m.start()
        flights[k] = made

    def settle(k):
        for m in flights[k]:
            m.wait_recv()
        for first in (0, 1024):
            c = pl.ds(first + 256 * k, 256)
            dact[:128, pl.ds(1024 + first + 256 * k, 256)] = (edge[:, c] + hin[:, c].astype(jnp.float32)).astype(bf)
        for which in range(3):
            mine = pl.ds(pl.multiple_of(which * 1024 + (2 * k + me.c) * 128, 128), 128)
            his = pl.ds(pl.multiple_of(which * 1024 + (2 * k + 1 - me.c) * 128, 128), 128)
            dcat[:, which * 128:which * 128 + 128] = dact[:, mine]
            dcat[:, 384 + which * 128:512 + which * 128] = dact[:, his]

        @pl.loop(0, 4)
        def _(i):
            r = pl.ds(pl.multiple_of(i * 256, 256), 256)
            t = nn(n0t[r, :], dcat[...]).astype(bf)
            acc1[r, k * 384:k * 384 + 384] = t[:, :384]
            outbox[r, k * 384:k * 384 + 384] = t[:, 384:]

    def send_terms(k):
        for which in range(3):
            at = k * 384 + which * 128
            line.launch(Reduce(me, sems, outbox.at[:, pl.ds(at, 128)], acc1, in1, co1, t1, 128, at,
                               which * 1024 + (2 * k + me.c) * 128, rotated(which + 3 * (k % 2))))

    def back_to_normed():
        @pl.loop(0, 4)
        def _(i):
            r = pl.ds(pl.multiple_of(i * 256, 256), 256)
            dn[:, r] = nt(dact[...], w1[r, :])

    def back_to_frames():
        @pl.loop(0, 6)
        def _(i):
            r = pl.ds(pl.multiple_of(i * 64, 64), 64)
            x = x0[r, :].astype(jnp.float32)
            inverse = inv[r, :]
            dframes[r, :] = (dh[r, :].astype(jnp.float32) + norm_backward(x, inverse, dn[r, :])).astype(bf)

    line.work(lambda: attend(0), 4.0)
    for k in range(1, 4):
        line.work(lambda: attend(k), 4.0)
        line.work(lambda: settle(k - 1), 1.2)
        send_terms(k - 1)
    line.work(lambda: settle(3), 1.2)
    send_terms(3)
    line.work(back_to_normed, 3.5)
    line.work(back_to_frames, 1.0)
    line.drain()
    for made in flights.values():
        for m in made:
            m.wait_send()


def last_part(*args):
    bf, f32 = jnp.bfloat16, jnp.float32
    v, h = pl.BlockSpec(memory_space=pltpu.VMEM), pl.BlockSpec(memory_space=pl.ANY)
    s = lambda shape, dt=bf: pltpu.VMEM(shape, dt)
    sizes = (3072, 1024, 3072, 1024)
    scratch = [s((1024, c // 2)) for _ in range(3) for c in sizes]
    scratch += [s((1024, 1536)), s((512, 128)), s((512, 128)), s((3, 384, 128), f32), s((512, 128), f32), s((512, 128), f32),
                s((128, 2048), f32), s((128, 2048)), s((128, 2048)), s((384, 3072)), s((384, 768)), s((384, 1024), f32),
                pltpu.SemaphoreType.DMA((520,)), pltpu.SemaphoreType.DMA((520,)), pltpu.SemaphoreType.DMA((3,))]
    return pl.pallas_call(
        last_kernel,
        out_shape=[jax.ShapeDtypeStruct((384, 1024), bf)] + [jax.ShapeDtypeStruct((256, c), bf) for c in sizes],
        in_specs=[h] * 3 + [v] * 10, out_specs=[v] * 5, scratch_shapes=scratch,
        compiler_params=pltpu.CompilerParams(collective_id=2, has_side_effects=True, vmem_limit_bytes=60 << 20),
        name="last_part",
    )(*args)


EPS = 1e-06
DEAD = 1 << 20


def normalize_rows(xfull):
    inverse = lax.rsqrt(jnp.mean(xfull * xfull, axis=-1, keepdims=True) + EPS)
    return (xfull * inverse, inverse)


def norm_backward(xfull, inverse, d_normed):
    row_inner = jnp.mean(d_normed * xfull, axis=-1, keepdims=True)
    return inverse * d_normed - xfull * (inverse * inverse * inverse) * row_inner


def shift(block, distance):
    n = lax.axis_size("seq")
    return lax.ppermute(block, "seq", [(i - distance, i) for i in range(n) if 0 <= i - distance < n])


def term(left, right):
    return lax.dot_general(left, right, (((0,), (0,)), ((), ())), preferred_element_type=jnp.float32).astype(jnp.bfloat16)


def local(frames, valid_length, span_frames, w1_shard, p1_shard, w2_shard, p2_shard, cotangent):
    bf, f32 = jnp.bfloat16, jnp.float32
    x0, cot = frames[0], cotangent[0]
    length, span = valid_length[0], span_frames[0]
    first = lax.axis_index("seq") * 384
    here = first + jnp.arange(384, dtype=jnp.int32)
    query_span = (here // span)[None, :]
    live = (here < length).astype(f32)[:, None]

    def key_span(positions):
        alive = (positions >= 0) & (positions < length)
        return jnp.where(alive, positions // span, DEAD)[:, None]

    ahead_span = key_span(first + jnp.arange(512, dtype=jnp.int32))
    behind_span = key_span(first - 192 + jnp.arange(576, dtype=jnp.int32))

    w1, p1, w2, p2 = gather_weights(w1_shard, p1_shard, w2_shard, p2_shard)

    x0f = x0.astype(f32)
    n0f, inv0 = normalize_rows(x0f)
    n0 = n0f.astype(bf)
    act1 = nn(n0, w1).astype(bf)
    halo1 = shift(act1[:128, 1024:], -1)
    (mix1,) = attention_call(up_forward_kernel, 128, "up_forward", act1, halo1, None, query_span, ahead_span, live, True, False)
    hidden = (x0f + nn(mix1, p1)).astype(bf)
    hf = hidden.astype(f32)
    n1f, inv1 = normalize_rows(hf)
    n1 = n1f.astype(bf)
    act2 = nn(n1, w2).astype(bf)
    halo2 = shift(act2[192:, 1024:], 1)
    dmix2 = (nt(cot, p2) * live).astype(bf)
    mix2, dq2, dk2, dv2, dkh2, dvh2 = attention_call(
        dit_kernel, 192, "dit", act2, halo2, dmix2, query_span, behind_span, live, True, True)
    result = (hf + nn(mix2, p2)).astype(bf)
    gp2 = term(mix2, cot)
    back2 = shift(jnp.concatenate([dkh2, dvh2], axis=1), -1).astype(f32)
    late = jnp.pad(back2, ((192, 0), (0, 0)))
    dact2 = jnp.concatenate([dq2, (dk2 + late[:, :1024]).astype(bf), (dv2 + late[:, 1024:]).astype(bf)], axis=1)
    gw2 = term(n1, dact2)
    dhidden = (cot.astype(f32) + norm_backward(hf, inv1, nt(dact2, w2))).astype(bf)
    dmix1 = (nt(dhidden, p1) * live).astype(bf)
    gp1 = term(mix1, dhidden)
    scale = float(8 * 6144) ** -0.5
    dframes, *totals = last_part(gp2, gw2, gp1, act1, halo1, dmix1, dhidden, x0, inv0, n0.T, w1, query_span, ahead_span)
    return (result[None], dframes[None], *(t.astype(f32) * scale for t in totals))


def solution(mesh):
    rows3, row, flat = P(("fsdp", "dp"), "seq", None), P("fsdp", None), P(("fsdp", "dp"))
    return jax.shard_map(
        local, mesh=mesh, in_specs=(rows3, flat, flat, row, row, row, row, rows3),
        out_specs=(rows3, rows3, row, row, row, row), check_vma=False)
```

```python
import functools
import heapq
import jax
import jax.numpy as jnp
from jax import lax
from jax.experimental import pallas as pl
from jax.experimental.pallas import tpu as pltpu
from jax.sharding import PartitionSpec as P

LINKS = ("xA", "yB", "zA", "xB", "yA", "zB")
PLANE = ("xA", "zA", "xB", "zB")


class Place:
    def __init__(self):
        seq = lax.axis_index("seq")
        self.seq = seq
        self.y = lax.axis_index("fsdp")
        self.zl = lax.axis_index("dp")
        self.x = seq // 4
        self.zh = (seq // 2) % 2
        self.c = seq % 2
        self.z = self.zh * 2 + self.zl

    def bit(self, link):
        p = {"x": self.x, "y": self.y, "z": self.z}[link[0]]
        return ((p + 1) // 2) % 2 if link[1] == "A" else p // 2

    def peer(self, link):
        x, y, z, c = self.x, self.y, self.z, self.c
        if link == "core":
            c = 1 - c
        elif link in ("next", "previous"):
            pass
        elif link[0] == "x":
            x = 3 - x if link[1] == "B" else x + 1 - 2 * (x % 2)
        elif link[0] == "y":
            y = 3 - y if link[1] == "B" else y + 1 - 2 * (y % 2)
        else:
            z = 3 - z if link[1] == "B" else z + 1 - 2 * (z % 2)
        if link == "next":
            return {"seq": (self.seq + 1) % 16, "fsdp": y, "dp": self.zl}
        if link == "previous":
            return {"seq": (self.seq + 15) % 16, "fsdp": y, "dp": self.zl}
        return {"seq": x * 4 + (z // 2) * 2 + c, "fsdp": y, "dp": z % 2}


def greet(me, *more):
    barrier = pltpu.get_barrier_semaphore()
    for link in LINKS + ("core",) + more:
        pl.semaphore_signal(barrier, inc=1, device_id=me.peer(link), device_id_type=pl.DeviceIdType.MESH)
    pl.semaphore_wait(barrier, 7 + len(more))


class Sems:
    def __init__(self, send, recv):
        self.send, self.recv, self.n = send, recv, 0

    def copy(self, me, link, src, dst):
        k = self.n
        self.n += 1
        return pltpu.make_async_remote_copy(
            src_ref=src, dst_ref=dst, send_sem=self.send.at[k], recv_sem=self.recv.at[k],
            device_id=me.peer(link), device_id_type=pl.DeviceIdType.MESH)


def rows(block, off, count):
    return pl.ds(pl.multiple_of(block * 256 + off, 16), count)


class Gather:
    def __init__(self, me, sems, shard, full, width, at, order):
        self.me, self.sems, self.shard, self.full, self.order = me, sems, shard, full, order
        self.cols = pl.ds(pl.multiple_of(at, 128), width)
        self.width = width
        self.sent = []
        y = me.y
        self.a, self.b = y + 1 - 2 * (y % 2), 3 - y
        self.ab = 3 - self.a
        self.steps = len(order) + 1
        self.span = 16 if len(order) > 2 else 256
        self.off = 0
        if len(order) > 2:
            for k, link in enumerate(order[2:]):
                self.off = self.off + me.bit(link) * (16 << k)
        self.wait_for = []

    def own(self):
        return self.shard.at[pl.ds(pl.multiple_of(self.off + 0, 16), self.span), self.cols]

    def blk(self, block):
        return self.full.at[rows(block, self.off, self.span), self.cols]

    def _go(self, link, pairs):
        made = [self.sems.copy(self.me, link, s, d) for s, d in pairs]
        for m in made:
            m.start()
        self.sent += made
        self.wait_for = made

    def start(self, step):
        me = self.me
        if step < 2:
            link = self.order[step]
            pairs = [(self.own(), self.blk(me.y))]
            if step == 1:
                other = self.a if self.order[0] == "yA" else self.b
                pairs.append((self.blk(other), self.blk(other)))
            self._go(link, pairs)
        elif step < len(self.order):
            self._go(self.order[step], [(self.blk(k), self.blk(k)) for k in (self.a, self.b, self.ab)])
        else:
            self._go("core", [(self.blk(k), self.blk(k)) for k in (self.a, self.b, self.ab)])

    def load(self, step):
        blocks = 1 if step == 0 else 2 if step == 1 else 3
        return (self.order + ("core",))[step], blocks * self.span * self.width * 2, 0.0

    def finish(self, step):
        for m in self.wait_for:
            m.wait_recv()
        if 2 <= step < len(self.order):
            link = self.order[step]
            self.off = self.off - self.me.bit(link) * self.span
            self.span *= 2

    def close(self):
        for m in self.sent:
            m.wait_send()


class Reduce:
    def __init__(self, me, sems, source, acc, inbox, inbox_core, gat, width, at, gat_at, order, ready=None):
        self.me, self.sems, self.source, self.acc, self.inbox, self.inbox_core, self.gat = me, sems, source, acc, inbox, inbox_core, gat
        self.width, self.order, self.ready = width, order, ready
        self.back = tuple(l for l in reversed(order) if l[0] != "y")
        self.cols = pl.ds(at, width)
        self.mine = pl.ds(pl.multiple_of(gat_at, 128), width)
        self.sent = []
        y = me.y
        a, b = y + 1 - 2 * (y % 2), 3 - y
        self.y, self.a, self.b, self.ab = y, a, b, 3 - a
        self.live = None
        self.off, self.span, self.inbox_at = 0, 256, 0
        self.steps = 12
        self.left = 1024

    def _go(self, link, pairs):
        made = [self.sems.copy(self.me, link, s, d) for s, d in pairs]
        for m in made:
            m.start()
        self.sent += made
        self.wait_for = made

    def load(self, step):
        line = 2 * self.width
        if step == 0:
            return "core", 1024 * line, 1024 * line / 1.5e6
        if step <= 6:
            return self.order[step - 1], (512 >> (step - 1)) * line, (512 >> (step - 1)) * line / 1.5e6 + 0.1
        if step <= 10:
            return self.back[step - 7], (16 << (step - 7)) * line, 0.0
        return "core", 256 * line, 0.0

    def start(self, step):
        me = self.me
        if step == 0:
            self._go("core", [(self.source, self.inbox_core.at[:, self.cols])])
        elif step <= 6:
            link = self.order[step - 1]
            bit = me.bit(link)
            if link[0] == "y":
                y, a, b, ab = self.y, self.a, self.b, self.ab
                if self.live is None:
                    keep, send = ([y, b], [a, ab]) if link[1] == "A" else ([y, a], [b, ab])
                else:
                    keep, send = [y], [a if link[1] == "A" else b]
                self.live = keep
                keep_off = send_off = self.off
            else:
                self.span //= 2
                keep = send = [0, 1, 2, 3] if self.live is None else self.live
                keep_off = self.off + bit * self.span
                send_off = self.off + (1 - bit) * self.span
                self.off = keep_off
            pairs, self.adds = [], []
            for k, s in zip(keep, send, strict=True):
                box = pl.ds(self.inbox_at, self.span)
                pairs.append((self.acc.at[rows(s, send_off, self.span), self.cols], self.inbox.at[box, self.cols]))
                self.adds.append((k * 256 + keep_off, self.inbox_at, self.span))
                self.inbox_at += self.span
            self._go(link, pairs)
        elif step <= 10:
            here = self.gat.at[pl.ds(pl.multiple_of(self.off, 16), self.span), self.mine]
            self._go(self.back[step - 7], [(here, here)])
        else:
            here = self.gat.at[:, self.mine]
            self._go("core", [(here, here)])

    def finish(self, step):
        for m in self.wait_for:
            m.wait_recv()
        if step == 0:
            if self.ready is not None:
                self.ready()

            @pl.loop(0, 1024 // 64)
            def _(i):
                r = pl.ds(pl.multiple_of(i * 64, 64), 64)
                self.acc[r, self.cols] = self.acc[r, self.cols] + self.inbox_core[r, self.cols]
        elif step <= 6:
            for at, box, count in self.adds:
                chunk = min(count, 64)

                @pl.loop(0, count // chunk)
                def _(i):
                    r = pl.ds(pl.multiple_of(at + i * chunk, 16), chunk)
                    q = pl.ds(pl.multiple_of(box + i * chunk, 16), chunk)
                    self.acc[r, self.cols] = self.acc[r, self.cols] + self.inbox[q, self.cols]
            if step == 6:
                self.gat[pl.ds(pl.multiple_of(self.off, 16), self.span), self.mine] = self.acc[
                    rows(self.y, self.off, self.span), self.cols]
        elif step <= 10:
            self.off = self.off - self.me.bit(self.back[step - 7]) * self.span
            self.span *= 2

    def close(self):
        for m in self.sent:
            m.wait_send()


class Timeline:
    def __init__(self):
        self.now, self.free, self.queue, self.count, self.parts = 0.0, {}, [], 0, []

    def launch(self, part, step=0):
        if step == 0:
            self.parts.append(part)
            part.over = False
        link, size, cost = part.load(step)
        part.start(step)
        begin = max(self.now, self.free.get(link, 0.0))
        end = begin + size / (0.55e6 if link == "core" else 0.046e6)
        self.free[link] = end
        heapq.heappush(self.queue, (end + (1.0 if link == "core" else 2.0), self.count, part, step, cost))
        self.count += 1

    def _one(self):
        end, _, part, step, cost = heapq.heappop(self.queue)
        self.now = max(self.now, end)
        part.finish(step)
        part.over = step + 1 == part.steps
        self.now += cost
        if step + 1 < part.steps:
            self.launch(part, step + 1)

    def poll(self):
        while self.queue and self.queue[0][0] <= self.now:
            self._one()

    def work(self, what, time):
        what()
        self.now += time
        self.poll()

    def until(self, parts):
        while any(not p.over for p in parts):
            self._one()

    def drain(self):
        while self.queue:
            self._one()
        for part in self.parts:
            part.close()


def rotated(i):
    return tuple(LINKS[(i + j) % 6] for j in range(6))


def reduce_parts(me, sems, terms, acc, inbox, inbox_core, gat, ready):
    columns = terms.shape[1]
    half = columns // 2
    n, starts = (6, (0, 1, 2, 3, 4, 5)) if columns == 3072 else (4, (0, 1, 3, 4))
    width = half // n
    out = []
    for i in range(n):
        source = terms.at[:, pl.ds(pl.multiple_of((1 - me.c) * half + i * width, 128), width)]
        out.append(Reduce(me, sems, source, acc, inbox, inbox_core, gat, width, i * width, me.c * half + i * width,
                          rotated(starts[i]), ready if i == 0 else None))
    return out


def gather_parts(me, sems, shard, full):
    cols = full.shape[1]
    half = cols // 2
    tiles = half // 128
    plans = []
    planes = [tuple(PLANE[(i + j) % 4] for j in range(4)) for i in range(4)]
    if tiles == 12:
        at = 0
        for i in range(4):
            plans.append((256, at, (("yA", "yB") if i % 2 else ("yB", "yA")) + planes[i]))
            at += 256
        plans.append((256, at, ("yA", "yB")))
        plans.append((256, at + 256, ("yB", "yA")))
    else:
        for i in range(4):
            plans.append((128, i * 128, (("yA", "yB") if i % 2 else ("yB", "yA")) + planes[i]))
    return [Gather(me, sems, shard, full, w, me.c * half + at, order) for w, at, order in plans]


FAR = -1e30


def heads_apart(block):
    first = lax.broadcasted_iota(jnp.int32, block.shape, 1) < 64
    zero = jnp.zeros_like(block)
    return jnp.concatenate([jnp.where(first, block, zero), jnp.where(first, zero, block)], axis=0)


def heads_together(wide):
    count = wide.shape[1] // 2
    return jnp.concatenate([wide[:64, :count], wide[64:, count:]], axis=0).T


def nt(a, b):
    return lax.dot_general(a, b, (((1,), (1,)), ((), ())), preferred_element_type=jnp.float32)


def tn(a, b):
    return lax.dot_general(a, b, (((0,), (0,)), ((), ())), preferred_element_type=jnp.float32)


def nn(a, b):
    return jnp.dot(a, b, preferred_element_type=jnp.float32)


def window_bias(key_span, query_span, low, high):
    gap = key_span - query_span
    return jnp.where((gap >= low) & (gap <= high), 0.0, FAR).astype(jnp.float32)


def prob_of(keys, queries, bias):
    score = nt(keys, queries) + jnp.concatenate([bias, bias], axis=1)
    terms = jnp.exp(score - jnp.max(score, axis=0, keepdims=True))
    return terms * (1.0 / jnp.sum(terms, axis=0, keepdims=True))


UP_BLOCKS = ((0, 0, 256), (128, 64, 320), (256, 192, 320))
DIT_BLOCKS = ((0, 0, 384), (128, 128, 384), (256, 256, 320))


def first_kernel(x0, cot, s0, s1, s2, s3, qs, ahead, behind, live,
                 act1, halo1, n0t, inv0, n1t, dact, mix1, mix2, result, dh, dmix1, w1_out,
                 w1, p1, w2, p2, n0, n1, inv1, hidden, act2, halo2, dmix2, dn, sums, hout, hin, bias1, bias2, send, recv, local):
    me = Place()
    bf, f32 = jnp.bfloat16, jnp.float32
    sems = Sems(send, recv)
    shards, fulls = (s0, s1, s2, s3), (w1, p1, w2, p2)
    own = [pltpu.make_async_copy(s, f.at[rows(me.y, 0, 256), :], local.at[i]) for i, (s, f) in enumerate(zip(shards, fulls, strict=True))]
    for cp in own:
        cp.start()
    greet(me, "next", "previous")
    line = Timeline()
    parts = [gather_parts(me, sems, s, f) for s, f in zip(shards, fulls, strict=True)]

    def fetch(i):
        for part in parts[i]:
            line.launch(part)

    def have(i):
        line.until(parts[i])
        own[i].wait()

    def chunks(count, width):
        def run(body):
            @pl.loop(0, count)
            def _(i):
                body(pl.ds(pl.multiple_of(i * width, width), width))
        return run

    def normalize(source, normed, inverse):
        @chunks(6, 64)
        def _(r):
            value, inv = normalize_rows(source[r, :].astype(f32))
            normed[r, :] = value.astype(bf)
            inverse[r, :] = inv

    def turn(normed, turned):
        @chunks(4, 256)
        def _(c):
            turned[c, :] = normed[:, c].T

    def project(normed, weight, act, low, high):
        @pl.loop(low, high)
        def _(i):
            c = pl.ds(pl.multiple_of(i * 512, 512), 512)
            act[:, c] = nn(normed[...], weight[:, c]).astype(bf)

    def heads(k, body):
        @pl.loop(2 * k, 2 * k + 2)
        def _(g):
            at = pl.multiple_of(g * 128, 128)
            body(pl.ds(at, 128), pl.ds(at + 1024, 128), pl.ds(at + 2048, 128))

    def up_block(i, q_at, k_at, v_at):
        r0, k0, n = UP_BLOCKS[i]
        keys, values = act1[k0:min(k0 + n, 384), k_at], act1[k0:min(k0 + n, 384), v_at]
        if i == 2:
            keys = jnp.concatenate([keys, halo1[:, q_at]], axis=0)
            values = jnp.concatenate([values, halo1[:, k_at]], axis=0)
        queries = heads_apart(act1[r0:r0 + 128, q_at] * jnp.bfloat16(0.125))
        p = prob_of(keys, queries, bias1[i, :n])
        mix1[r0:r0 + 128, q_at] = (heads_together(tn(values, p.astype(bf))) * live[r0:r0 + 128]).astype(bf)

    def up_early(k):
        def body(*at):
            up_block(0, *at)
            up_block(1, *at)
        heads(k, body)

    def up_late(k):
        heads(k, lambda *at: up_block(2, *at))

    def dit_block(i, q_at, k_at, v_at):
        r0, k0, n = DIT_BLOCKS[i]
        keys, values = act2[max(k0 - 192, 0):k0 - 192 + n, k_at], act2[max(k0 - 192, 0):k0 - 192 + n, v_at]
        if k0 < 192:
            keys = jnp.concatenate([halo2[k0:, q_at], keys], axis=0)
            values = jnp.concatenate([halo2[k0:, k_at], values], axis=0)
        queries = heads_apart(act2[r0:r0 + 128, q_at] * jnp.bfloat16(0.125))
        p = prob_of(keys, queries, bias2[i, :n])
        low = p.astype(bf)
        mix2[r0:r0 + 128, q_at] = (heads_together(tn(values, low)) * live[r0:r0 + 128]).astype(bf)
        dout = heads_apart(dmix2[r0:r0 + 128, q_at])
        dp = nt(values, dout)
        ds = (p * (dp - jnp.sum(p * dp, axis=0, keepdims=True))).astype(bf)
        dact[r0:r0 + 128, q_at] = (heads_together(tn(keys, ds)) * 0.125).astype(bf)
        return nn(ds, queries), nn(low, dout)

    def dit_early(k):
        def body(q_at, k_at, v_at):
            dk, dv = dit_block(2, q_at, k_at, v_at)
            for at, d in ((q_at, dk), (k_at, dv)):
                sums[:256, at] = jnp.zeros((256, 128), f32)
                sums[256:, at] = d
        heads(k, body)

    flights = {}

    def dit_late(k):
        def body(q_at, k_at, v_at):
            for i in (0, 1):
                _, k0, n = DIT_BLOCKS[i]
                dk, dv = dit_block(i, q_at, k_at, v_at)
                sums[k0:k0 + n, q_at] += dk
                sums[k0:k0 + n, k_at] += dv
            for at, to in ((q_at, k_at), (k_at, v_at)):
                hout[:, at] = sums[:192, at].astype(bf)
                dact[:192, to] = sums[192:384, at].astype(bf)
        heads(k, body)
        flights[k] = [sems.copy(me, "previous", hout.at[:, c], hin.at[:, c]) for c in (pl.ds(256 * k, 256), pl.ds(1024 + 256 * k, 256))]
        for m in flights[k]:
            m.start()

    def settle(k):
        for m in flights[k]:
            m.wait_recv()
        for first in (256 * k, 1024 + 256 * k):
            c = pl.ds(first, 256)
            dact[192:, pl.ds(1024 + first, 256)] = (sums[384:, c] + hin[:, c].astype(f32)).astype(bf)

    def mixed_back(grad, weight, out):
        @chunks(4, 256)
        def _(c):
            out[:, c] = (nt(grad[...], weight[c, :]) * live[...]).astype(bf)

    def add_mixed(base, mix, weight, out):
        @chunks(4, 256)
        def _(c):
            out[:, c] = (base[:, c].astype(f32) + nn(mix[...], weight[:, c])).astype(bf)

    def normed_back():
        @chunks(4, 256)
        def _(c):
            dn[:, c] = nt(dact[...], w2[c, :])

    def hidden_back():
        @chunks(6, 64)
        def _(r):
            dh[r, :] = (cot[r, :].astype(f32) + norm_backward(hidden[r, :].astype(f32), inv1[r, :], dn[r, :])).astype(bf)

    def biases():
        for i, (r0, k0, n) in enumerate(UP_BLOCKS):
            bias1[i, :n] = window_bias(ahead[k0:k0 + n], qs[:, r0:r0 + 128], 0, 1)
        for i, (r0, k0, n) in enumerate(DIT_BLOCKS):
            bias2[i, :n] = window_bias(behind[k0:k0 + n], qs[:, r0:r0 + 128], -2, 0)

    fetch(0)
    fetch(1)
    line.work(lambda: normalize(x0, n0, inv0), 1.5)
    line.work(biases, 0.7)
    fetch(2)
    line.work(lambda: turn(n0, n0t), 0.8)
    have(0)
    fetch(3)
    keep = pltpu.make_async_copy(w1, w1_out, local.at[4])
    keep.start()
    line.work(lambda: project(n0, w1, act1, 2, 6), 2.0)
    give1 = sems.copy(me, "previous", act1.at[pl.ds(0, 128), pl.ds(1024, 2048)], halo1)
    give1.start()
    line.work(lambda: project(n0, w1, act1, 0, 2), 1.0)
    for k in range(4):
        line.work(lambda: up_early(k), 1.5)
    give1.wait_recv()
    for k in range(4):
        line.work(lambda: up_late(k), 0.9)
    have(1)
    line.work(lambda: add_mixed(x0, mix1, p1, hidden), 1.0)
    line.work(lambda: normalize(hidden, n1, inv1), 1.2)
    have(2)
    line.work(lambda: project(n1, w2, act2, 2, 6), 2.0)
    give2 = sems.copy(me, "next", act2.at[pl.ds(192, 192), pl.ds(1024, 2048)], halo2)
    give2.start()
    line.work(lambda: project(n1, w2, act2, 0, 2), 1.0)
    have(3)
    line.work(lambda: mixed_back(cot, p2, dmix2), 1.0)
    line.drain()
    for k in range(4):
        dit_early(k)
    turn(n1, n1t)
    give2.wait_recv()
    for k in range(4):
        dit_late(k)
        if k:
            settle(k - 1)
    add_mixed(hidden, mix2, p2, result)
    settle(3)
    normed_back()
    hidden_back()
    mixed_back(dh, p1, dmix1)
    keep.wait()
    for m in [give1, give2] + [m for made in flights.values() for m in made]:
        m.wait_send()


def first_part(*args):
    bf, f32 = jnp.bfloat16, jnp.float32
    v, h = pl.BlockSpec(memory_space=pltpu.VMEM), pl.BlockSpec(memory_space=pl.ANY)
    s = lambda shape, dt=bf: pltpu.VMEM(shape, dt)
    o = lambda *shape, dt=bf: jax.ShapeDtypeStruct(shape, dt)
    scratch = [s((1024, 3072)), s((1024, 1024)), s((1024, 3072)), s((1024, 1024)), s((384, 1024)), s((384, 1024)), s((384, 1), f32),
               s((384, 1024)), s((384, 3072)), s((192, 2048)), s((384, 1024)), s((384, 1024), f32), s((576, 2048), f32),
               s((192, 2048)), s((192, 2048)), s((3, 384, 128), f32), s((3, 384, 128), f32),
               pltpu.SemaphoreType.DMA((400,)), pltpu.SemaphoreType.DMA((400,)), pltpu.SemaphoreType.DMA((5,))]
    return pl.pallas_call(
        first_kernel,
        out_shape=[o(384, 3072), o(128, 2048), o(1024, 384), o(384, 1, dt=f32), o(1024, 384), o(384, 3072)] + [o(384, 1024)] * 5 + [o(1024, 3072)],
        in_specs=[v] * 2 + [h] * 4 + [v] * 4, out_specs=[v] * 11 + [h], scratch_shapes=scratch,
        compiler_params=pltpu.CompilerParams(collective_id=1, has_side_effects=True, vmem_limit_bytes=60 << 20),
        name="first_part",
    )(*args)


def last_kernel(gp2, gw2, gp1, act, halo, dm, dh, x0, inv, n0t, w1, qs, ks,
                dframes, t1, tp1, t2, tp2,
                acc1, accp1, acc2, accp2, in1, inp1, in2, inp2, co1, cop1, co2, cop2,
                outbox, kx, vx, bias, dkx, dvx, edge, hout, hin, dact, dcat, dn, send, recv, local):
    me = Place()
    bf = jnp.bfloat16
    sems = Sems(send, recv)
    loads = []
    for i, (t, acc) in enumerate(((gp2, accp2), (gw2, acc2), (gp1, accp1))):
        half = t.shape[1] // 2
        cp = pltpu.make_async_copy(t.at[:, pl.ds(pl.multiple_of(me.c * half, 128), half)], acc, local.at[i])
        cp.start()
        loads.append(cp)
    for i, (r0, k0, n) in enumerate(UP_BLOCKS):
        bias[i, :n] = window_bias(ks[k0:k0 + n], qs[:, r0:r0 + 128], 0, 1)
    greet(me, "next", "previous")
    line = Timeline()
    for i, (t, acc, box, core, gat) in enumerate(((gp2, accp2, inp2, cop2, tp2), (gw2, acc2, in2, co2, t2), (gp1, accp1, inp1, cop1, tp1))):
        for part in reduce_parts(me, sems, t, acc, box, core, gat, loads[i].wait):
            line.launch(part)

    flights = {}

    def attend(k):
        @pl.loop(2 * k, 2 * k + 2)
        def _(g):
            at = pl.multiple_of(g * 128, 128)
            q_at, k_at, v_at = pl.ds(at, 128), pl.ds(at + 1024, 128), pl.ds(at + 2048, 128)
            kx[:384], kx[384:] = act[:, k_at], halo[:, q_at]
            vx[:384], vx[384:] = act[:, v_at], halo[:, k_at]
            dkx[...] = jnp.zeros_like(dkx)
            dvx[...] = jnp.zeros_like(dvx)
            for i, (r0, k0, n) in enumerate(UP_BLOCKS):
                keys, values = kx[k0:k0 + n], vx[k0:k0 + n]
                queries = heads_apart(act[r0:r0 + 128, q_at] * jnp.bfloat16(0.125))
                p = prob_of(keys, queries, bias[i, :n])
                dout = heads_apart(dm[r0:r0 + 128, q_at])
                dp = nt(values, dout)
                ds = (p * (dp - jnp.sum(p * dp, axis=0, keepdims=True))).astype(bf)
                dvx[k0:k0 + n] += nn(p.astype(bf), dout)
                dkx[k0:k0 + n] += nn(ds, queries)
                dact[r0:r0 + 128, q_at] = (heads_together(tn(keys, ds)) * 0.125).astype(bf)
            for full, c_at, e_at in ((dkx, k_at, q_at), (dvx, v_at, k_at)):
                edge[:, e_at] = full[:128]
                dact[128:, c_at] = full[128:384].astype(bf)
                hout[:, e_at] = full[384:].astype(bf)

        made = []
        for first in (0, 1024):
            c = pl.ds(first + 256 * k, 256)
            made.append(sems.copy(me, "next", hout.at[:, c], hin.at[:, c]))
        for m in made:
            m.start()
        flights[k] = made

    def settle(k):
        for m in flights[k]:
            m.wait_recv()
        for first in (0, 1024):
            c = pl.ds(first + 256 * k, 256)
            dact[:128, pl.ds(1024 + first + 256 * k, 256)] = (edge[:, c] + hin[:, c].astype(jnp.float32)).astype(bf)
        for which in range(3):
            mine = pl.ds(pl.multiple_of(which * 1024 + (2 * k + me.c) * 128, 128), 128)
            his = pl.ds(pl.multiple_of(which * 1024 + (2 * k + 1 - me.c) * 128, 128), 128)
            dcat[:, which * 128:which * 128 + 128] = dact[:, mine]
            dcat[:, 384 + which * 128:512 + which * 128] = dact[:, his]

        @pl.loop(0, 4)
        def _(i):
            r = pl.ds(pl.multiple_of(i * 256, 256), 256)
            t = nn(n0t[r, :], dcat[...]).astype(bf)
            acc1[r, k * 384:k * 384 + 384] = t[:, :384]
            outbox[r, k * 384:k * 384 + 384] = t[:, 384:]

    def send_terms(k):
        for which in range(3):
            at = k * 384 + which * 128
            line.launch(Reduce(me, sems, outbox.at[:, pl.ds(at, 128)], acc1, in1, co1, t1, 128, at,
                               which * 1024 + (2 * k + me.c) * 128, rotated(which + 3 * (k % 2))))

    def back_to_normed():
        @pl.loop(0, 4)
        def _(i):
            r = pl.ds(pl.multiple_of(i * 256, 256), 256)
            dn[:, r] = nt(dact[...], w1[r, :])

    def back_to_frames():
        @pl.loop(0, 6)
        def _(i):
            r = pl.ds(pl.multiple_of(i * 64, 64), 64)
            x = x0[r, :].astype(jnp.float32)
            inverse = inv[r, :]
            dframes[r, :] = (dh[r, :].astype(jnp.float32) + norm_backward(x, inverse, dn[r, :])).astype(bf)

    line.work(lambda: attend(0), 4.0)
    for k in range(1, 4):
        line.work(lambda: attend(k), 4.0)
        line.work(lambda: settle(k - 1), 1.2)
        send_terms(k - 1)
    line.work(lambda: settle(3), 1.2)
    send_terms(3)
    line.work(back_to_normed, 3.5)
    line.work(back_to_frames, 1.0)
    line.drain()
    for made in flights.values():
        for m in made:
            m.wait_send()


def last_part(*args):
    bf, f32 = jnp.bfloat16, jnp.float32
    v, h = pl.BlockSpec(memory_space=pltpu.VMEM), pl.BlockSpec(memory_space=pl.ANY)
    s = lambda shape, dt=bf: pltpu.VMEM(shape, dt)
    sizes = (3072, 1024, 3072, 1024)
    scratch = [s((1024, c // 2)) for _ in range(3) for c in sizes]
    scratch += [s((1024, 1536)), s((512, 128)), s((512, 128)), s((3, 384, 128), f32), s((512, 128), f32), s((512, 128), f32),
                s((128, 2048), f32), s((128, 2048)), s((128, 2048)), s((384, 3072)), s((384, 768)), s((384, 1024), f32),
                pltpu.SemaphoreType.DMA((520,)), pltpu.SemaphoreType.DMA((520,)), pltpu.SemaphoreType.DMA((3,))]
    return pl.pallas_call(
        last_kernel,
        out_shape=[jax.ShapeDtypeStruct((384, 1024), bf)] + [jax.ShapeDtypeStruct((256, c), bf) for c in sizes],
        in_specs=[h] * 3 + [v] * 10, out_specs=[v] * 5, scratch_shapes=scratch,
        compiler_params=pltpu.CompilerParams(collective_id=2, has_side_effects=True, vmem_limit_bytes=60 << 20),
        name="last_part",
    )(*args)


EPS = 1e-06
DEAD = 1 << 20


def normalize_rows(xfull):
    inverse = lax.rsqrt(jnp.mean(xfull * xfull, axis=-1, keepdims=True) + EPS)
    return (xfull * inverse, inverse)


def norm_backward(xfull, inverse, d_normed):
    row_inner = jnp.mean(d_normed * xfull, axis=-1, keepdims=True)
    return inverse * d_normed - xfull * (inverse * inverse * inverse) * row_inner


def term(left, right):
    return lax.dot_general(left, right, (((0,), (0,)), ((), ())), preferred_element_type=jnp.float32).astype(jnp.bfloat16)


def local(frames, valid_length, span_frames, w1_shard, p1_shard, w2_shard, p2_shard, cotangent):
    bf, f32 = jnp.bfloat16, jnp.float32
    x0, cot = frames[0], cotangent[0]
    length, span = valid_length[0], span_frames[0]
    first = lax.axis_index("seq") * 384
    here = first + jnp.arange(384, dtype=jnp.int32)
    query_span = (here // span)[None, :]
    live = (here < length).astype(f32)[:, None]

    def key_span(positions):
        alive = (positions >= 0) & (positions < length)
        return jnp.where(alive, positions // span, DEAD)[:, None]

    ahead_span = key_span(first + jnp.arange(512, dtype=jnp.int32))
    behind_span = key_span(first - 192 + jnp.arange(576, dtype=jnp.int32))

    act1, halo1, n0t, inv0, n1t, dact2, mix1, mix2, result, dhidden, dmix1, w1 = first_part(
        x0, cot, w1_shard, p1_shard, w2_shard, p2_shard, query_span, ahead_span, behind_span, live)
    gp2 = term(mix2, cot)
    gw2 = nn(n1t, dact2).astype(bf)
    gp1 = term(mix1, dhidden)
    scale = float(8 * 6144) ** -0.5
    dframes, *totals = last_part(gp2, gw2, gp1, act1, halo1, dmix1, dhidden, x0, inv0, n0t, w1, query_span, ahead_span)
    return (result[None], dframes[None], *(t.astype(f32) * scale for t in totals))


def solution(mesh):
    rows3, row, flat = P(("fsdp", "dp"), "seq", None), P("fsdp", None), P(("fsdp", "dp"))
    return jax.shard_map(
        local, mesh=mesh, in_specs=(rows3, flat, flat, row, row, row, row, rows3),
        out_specs=(rows3, rows3, row, row, row, row), check_vma=False)
```

```python
import functools
import heapq
import jax
import jax.numpy as jnp
from jax import lax
from jax.experimental import pallas as pl
from jax.experimental.pallas import tpu as pltpu
from jax.sharding import PartitionSpec as P

LINKS = ("xA", "yB", "zA", "xB", "yA", "zB")
PLANE = ("xA", "zA", "xB", "zB")


class Place:
    def __init__(self):
        seq = lax.axis_index("seq")
        self.seq = seq
        self.y = lax.axis_index("fsdp")
        self.zl = lax.axis_index("dp")
        self.x = seq // 4
        self.zh = (seq // 2) % 2
        self.c = seq % 2
        self.z = self.zh * 2 + self.zl

    def bit(self, link):
        p = {"x": self.x, "y": self.y, "z": self.z}[link[0]]
        return ((p + 1) // 2) % 2 if link[1] == "A" else p // 2

    def peer(self, link):
        x, y, z, c = self.x, self.y, self.z, self.c
        if link == "core":
            c = 1 - c
        elif link in ("next", "previous"):
            pass
        elif link[0] == "x":
            x = 3 - x if link[1] == "B" else x + 1 - 2 * (x % 2)
        elif link[0] == "y":
            y = 3 - y if link[1] == "B" else y + 1 - 2 * (y % 2)
        else:
            z = 3 - z if link[1] == "B" else z + 1 - 2 * (z % 2)
        if link == "next":
            return {"seq": (self.seq + 1) % 16, "fsdp": y, "dp": self.zl}
        if link == "previous":
            return {"seq": (self.seq + 15) % 16, "fsdp": y, "dp": self.zl}
        return {"seq": x * 4 + (z // 2) * 2 + c, "fsdp": y, "dp": z % 2}


def greet(me, *more):
    barrier = pltpu.get_barrier_semaphore()
    for link in LINKS + ("core",) + more:
        pl.semaphore_signal(barrier, inc=1, device_id=me.peer(link), device_id_type=pl.DeviceIdType.MESH)
    pl.semaphore_wait(barrier, 7 + len(more))


class Sems:
    def __init__(self, send, recv):
        self.send, self.recv, self.n = send, recv, 0

    def copy(self, me, link, src, dst):
        k = self.n
        self.n += 1
        return pltpu.make_async_remote_copy(
            src_ref=src, dst_ref=dst, send_sem=self.send.at[k], recv_sem=self.recv.at[k],
            device_id=me.peer(link), device_id_type=pl.DeviceIdType.MESH)


def rows(block, off, count):
    return pl.ds(pl.multiple_of(block * 256 + off, 16), count)


class Gather:
    def __init__(self, me, sems, shard, full, width, at, order):
        self.me, self.sems, self.shard, self.full, self.order = me, sems, shard, full, order
        self.cols = pl.ds(pl.multiple_of(at, 128), width)
        self.width = width
        self.sent = []
        y = me.y
        self.a, self.b = y + 1 - 2 * (y % 2), 3 - y
        self.ab = 3 - self.a
        self.steps = len(order) + 1
        self.span = 256 >> (len(order) - 2)
        self.off = 0
        for k, link in enumerate(order[2:]):
            self.off = self.off + me.bit(link) * (self.span << k)
        self.wait_for = []

    def own(self):
        return self.shard.at[pl.ds(pl.multiple_of(self.off + 0, 16), self.span), self.cols]

    def blk(self, block):
        return self.full.at[rows(block, self.off, self.span), self.cols]

    def _go(self, link, pairs):
        made = [self.sems.copy(self.me, link, s, d) for s, d in pairs]
        for m in made:
            m.start()
        self.sent += made
        self.wait_for = made

    def start(self, step):
        me = self.me
        if step < 2:
            link = self.order[step]
            pairs = [(self.own(), self.blk(me.y))]
            if step == 1:
                other = self.a if self.order[0] == "yA" else self.b
                pairs.append((self.blk(other), self.blk(other)))
            self._go(link, pairs)
        elif step < len(self.order):
            self._go(self.order[step], [(self.blk(k), self.blk(k)) for k in (self.a, self.b, self.ab)])
        else:
            self._go("core", [(self.blk(k), self.blk(k)) for k in (self.a, self.b, self.ab)])

    def load(self, step):
        blocks = 1 if step == 0 else 2 if step == 1 else 3
        return (self.order + ("core",))[step], blocks * self.span * self.width * 2, 0.0

    def finish(self, step):
        for m in self.wait_for:
            m.wait_recv()
        if 2 <= step < len(self.order):
            link = self.order[step]
            self.off = self.off - self.me.bit(link) * self.span
            self.span *= 2

    def close(self):
        for m in self.sent:
            m.wait_send()


class Reduce:
    def __init__(self, me, sems, source, acc, inbox, inbox_core, gat, width, at, gat_at, order, ready=None):
        self.me, self.sems, self.source, self.acc, self.inbox, self.inbox_core, self.gat = me, sems, source, acc, inbox, inbox_core, gat
        self.width, self.order, self.ready = width, order, ready
        self.back = tuple(l for l in reversed(order) if l[0] != "y")
        self.cols = pl.ds(at, width)
        self.mine = pl.ds(pl.multiple_of(gat_at, 128), width)
        self.sent = []
        y = me.y
        a, b = y + 1 - 2 * (y % 2), 3 - y
        self.y, self.a, self.b, self.ab = y, a, b, 3 - a
        self.live = None
        self.off, self.span, self.inbox_at = 0, 256, 0
        self.steps = 12
        self.left = 1024

    def _go(self, link, pairs):
        made = [self.sems.copy(self.me, link, s, d) for s, d in pairs]
        for m in made:
            m.start()
        self.sent += made
        self.wait_for = made

    def load(self, step):
        line = 2 * self.width
        if step == 0:
            return "core", 1024 * line, 1024 * line / 1.5e6
        if step <= 6:
            return self.order[step - 1], (512 >> (step - 1)) * line, (512 >> (step - 1)) * line / 1.5e6 + 0.1
        if step <= 10:
            return self.back[step - 7], (16 << (step - 7)) * line, 0.0
        return "core", 256 * line, 0.0

    def start(self, step):
        me = self.me
        if step == 0:
            self._go("core", [(self.source, self.inbox_core.at[:, self.cols])])
        elif step <= 6:
            link = self.order[step - 1]
            bit = me.bit(link)
            if link[0] == "y":
                y, a, b, ab = self.y, self.a, self.b, self.ab
                if self.live is None:
                    keep, send = ([y, b], [a, ab]) if link[1] == "A" else ([y, a], [b, ab])
                else:
                    keep, send = [y], [a if link[1] == "A" else b]
                self.live = keep
                keep_off = send_off = self.off
            else:
                self.span //= 2
                keep = send = [0, 1, 2, 3] if self.live is None else self.live
                keep_off = self.off + bit * self.span
                send_off = self.off + (1 - bit) * self.span
                self.off = keep_off
            pairs, self.adds = [], []
            for k, s in zip(keep, send, strict=True):
                box = pl.ds(self.inbox_at, self.span)
                pairs.append((self.acc.at[rows(s, send_off, self.span), self.cols], self.inbox.at[box, self.cols]))
                self.adds.append((k * 256 + keep_off, self.inbox_at, self.span))
                self.inbox_at += self.span
            self._go(link, pairs)
        elif step <= 10:
            here = self.gat.at[pl.ds(pl.multiple_of(self.off, 16), self.span), self.mine]
            self._go(self.back[step - 7], [(here, here)])
        else:
            here = self.gat.at[:, self.mine]
            self._go("core", [(here, here)])

    def finish(self, step):
        for m in self.wait_for:
            m.wait_recv()
        if step == 0:
            if self.ready is not None:
                self.ready()

            @pl.loop(0, 1024 // 64)
            def _(i):
                r = pl.ds(pl.multiple_of(i * 64, 64), 64)
                self.acc[r, self.cols] = self.acc[r, self.cols] + self.inbox_core[r, self.cols]
        elif step <= 6:
            for at, box, count in self.adds:
                chunk = min(count, 64)

                @pl.loop(0, count // chunk)
                def _(i):
                    r = pl.ds(pl.multiple_of(at + i * chunk, 16), chunk)
                    q = pl.ds(pl.multiple_of(box + i * chunk, 16), chunk)
                    self.acc[r, self.cols] = self.acc[r, self.cols] + self.inbox[q, self.cols]
            if step == 6:
                self.gat[pl.ds(pl.multiple_of(self.off, 16), self.span), self.mine] = self.acc[
                    rows(self.y, self.off, self.span), self.cols]
        elif step <= 10:
            self.off = self.off - self.me.bit(self.back[step - 7]) * self.span
            self.span *= 2

    def close(self):
        for m in self.sent:
            m.wait_send()


class Timeline:
    def __init__(self):
        self.now, self.free, self.queue, self.count, self.parts = 0.0, {}, [], 0, []

    def launch(self, part, step=0):
        if step == 0:
            self.parts.append(part)
            part.over, part.past = False, -1
        link, size, cost = part.load(step)
        part.start(step)
        begin = max(self.now, self.free.get(link, 0.0))
        end = begin + size / (0.55e6 if link == "core" else 0.046e6)
        self.free[link] = end
        heapq.heappush(self.queue, (end + (1.0 if link == "core" else 2.0), self.count, part, step, cost))
        self.count += 1

    def _one(self):
        end, _, part, step, cost = heapq.heappop(self.queue)
        self.now = max(self.now, end)
        part.finish(step)
        part.over, part.past = step + 1 == part.steps, step
        self.now += cost
        if step + 1 < part.steps:
            self.launch(part, step + 1)

    def poll(self):
        while self.queue and self.queue[0][0] <= self.now:
            self._one()

    def work(self, what, time):
        what()
        self.now += time
        self.poll()

    def until(self, parts, step=9):
        while any(not p.over and p.past < step for p in parts):
            self._one()

    def drain(self):
        while self.queue:
            self._one()
        for part in self.parts:
            part.close()


def rotated(i):
    return tuple(LINKS[(i + j) % 6] for j in range(6))


def reduce_parts(me, sems, terms, acc, inbox, inbox_core, gat, ready):
    columns = terms.shape[1]
    half = columns // 2
    n, starts = (6, (0, 1, 2, 3, 4, 5)) if columns == 3072 else (4, (0, 1, 3, 4))
    width = half // n
    out = []
    for i in range(n):
        source = terms.at[:, pl.ds(pl.multiple_of((1 - me.c) * half + i * width, 128), width)]
        out.append(Reduce(me, sems, source, acc, inbox, inbox_core, gat, width, i * width, me.c * half + i * width,
                          rotated(starts[i]), ready if i == 0 else None))
    return out


def gather_parts(me, sems, shard, full):
    half = full.shape[1] // 2
    width = half // 4
    orders = (("yA", "yB", "xA", "xB"), ("yB", "yA", "zA", "zB"), ("yA", "yB", "xB", "xA"), ("yB", "yA", "zB", "zA"))
    return [Gather(me, sems, shard, full, width, me.c * half + i * width, order) for i, order in enumerate(orders)]


FAR = -1e30


def heads_apart(block):
    first = lax.broadcasted_iota(jnp.int32, block.shape, 1) < 64
    zero = jnp.zeros_like(block)
    return jnp.concatenate([jnp.where(first, block, zero), jnp.where(first, zero, block)], axis=0)


def heads_together(wide):
    count = wide.shape[1] // 2
    return jnp.concatenate([wide[:64, :count], wide[64:, count:]], axis=0).T


def nt(a, b):
    return lax.dot_general(a, b, (((1,), (1,)), ((), ())), preferred_element_type=jnp.float32)


def tn(a, b):
    return lax.dot_general(a, b, (((0,), (0,)), ((), ())), preferred_element_type=jnp.float32)


def nn(a, b):
    return jnp.dot(a, b, preferred_element_type=jnp.float32)


def window_bias(key_span, query_span, low, high):
    gap = key_span - query_span
    return jnp.where((gap >= low) & (gap <= high), 0.0, FAR).astype(jnp.float32)


def prob_of(keys, queries, bias):
    score = nt(keys, queries) + jnp.concatenate([bias, bias], axis=1)
    terms = jnp.exp(score - jnp.max(score, axis=0, keepdims=True))
    return terms * (1.0 / jnp.sum(terms, axis=0, keepdims=True))


class Spans:
    def __init__(self, me, length, size):
        self.first, self.length = me.seq * 384, length[0]
        self.inverse = 1.0 / jnp.full((1, 1), size[0].astype(jnp.float32))

    def at(self, start, count, axis):
        shape = (count, 1) if axis == 0 else (1, count)
        return self.first + start + lax.broadcasted_iota(jnp.int32, shape, axis)

    def number(self, frames):
        return jnp.floor((frames.astype(jnp.float32) + 0.5) * self.inverse)

    def bias(self, query, key, count, low, high):
        frames = self.at(key, count, 0)
        alive = (frames >= 0) & (frames < self.length)
        return window_bias(jnp.where(alive, self.number(frames), 1e6), self.number(self.at(query, 128, 1)), low, high)


UP_BLOCKS = ((0, 0, 256), (128, 64, 320), (256, 192, 320))
DIT_BLOCKS = ((0, 0, 384), (128, 128, 384), (256, 256, 320))


def first_kernel(x0, cot, s0, s1, s2, s3, length, size,
                 act1, halo1, n0t, inv0, n1t, dact, mix1, mix2, result, dh, dmix1, w1_out,
                 w1, p1, w2, p2, n0, n1, inv1, hidden, act2, halo2, dmix2, dn, sums, hout, hin, bias1, bias2, live, send, recv, local):
    me = Place()
    spans = Spans(me, length, size)
    bf, f32 = jnp.bfloat16, jnp.float32
    sems = Sems(send, recv)
    shards, fulls = (s0, s1, s2, s3), (w1, p1, w2, p2)
    own = [pltpu.make_async_copy(s, f.at[rows(me.y, 0, 256), :], local.at[i]) for i, (s, f) in enumerate(zip(shards, fulls, strict=True))]
    for cp in own:
        cp.start()
    greet(me, "next", "previous")
    line = Timeline()
    parts = [gather_parts(me, sems, s, f) for s, f in zip(shards, fulls, strict=True)]

    def fetch(i):
        for part in parts[i]:
            line.launch(part)

    def have(i):
        line.until(parts[i])
        own[i].wait()

    def chunks(count, width):
        def run(body):
            @pl.loop(0, count)
            def _(i):
                body(pl.ds(pl.multiple_of(i * width, width), width))
        return run

    def normalize(source, normed, inverse):
        @chunks(6, 64)
        def _(r):
            value, inv = normalize_rows(source[r, :].astype(f32))
            normed[r, :] = value.astype(bf)
            inverse[r, :] = inv

    def turn(normed, turned):
        @chunks(4, 256)
        def _(c):
            turned[c, :] = normed[:, c].T

    def project(normed, weight, act, low, high):
        @pl.loop(low, high)
        def _(i):
            c = pl.ds(pl.multiple_of(i * 512, 512), 512)
            act[:, c] = nn(normed[...], weight[:, c]).astype(bf)

    def heads(k, body):
        @pl.loop(2 * k, 2 * k + 2)
        def _(g):
            at = pl.multiple_of(g * 128, 128)
            body(pl.ds(at, 128), pl.ds(at + 1024, 128), pl.ds(at + 2048, 128))

    def up_block(i, q_at, k_at, v_at):
        r0, k0, n = UP_BLOCKS[i]
        keys, values = act1[k0:min(k0 + n, 384), k_at], act1[k0:min(k0 + n, 384), v_at]
        if i == 2:
            keys = jnp.concatenate([keys, halo1[:, q_at]], axis=0)
            values = jnp.concatenate([values, halo1[:, k_at]], axis=0)
        queries = heads_apart(act1[r0:r0 + 128, q_at] * jnp.bfloat16(0.125))
        p = prob_of(keys, queries, bias1[i, :n])
        mix1[r0:r0 + 128, q_at] = (heads_together(tn(values, p.astype(bf))) * live[r0:r0 + 128]).astype(bf)

    def up_early(k):
        def body(*at):
            up_block(0, *at)
            up_block(1, *at)
        heads(k, body)

    def up_late(k):
        heads(k, lambda *at: up_block(2, *at))

    def dit_block(i, q_at, k_at, v_at):
        r0, k0, n = DIT_BLOCKS[i]
        keys, values = act2[max(k0 - 192, 0):k0 - 192 + n, k_at], act2[max(k0 - 192, 0):k0 - 192 + n, v_at]
        if k0 < 192:
            keys = jnp.concatenate([halo2[k0:, q_at], keys], axis=0)
            values = jnp.concatenate([halo2[k0:, k_at], values], axis=0)
        queries = heads_apart(act2[r0:r0 + 128, q_at] * jnp.bfloat16(0.125))
        p = prob_of(keys, queries, bias2[i, :n])
        low = p.astype(bf)
        mix2[r0:r0 + 128, q_at] = (heads_together(tn(values, low)) * live[r0:r0 + 128]).astype(bf)
        dout = heads_apart(dmix2[r0:r0 + 128, q_at])
        dp = nt(values, dout)
        ds = (p * (dp - jnp.sum(p * dp, axis=0, keepdims=True))).astype(bf)
        dact[r0:r0 + 128, q_at] = (heads_together(tn(keys, ds)) * 0.125).astype(bf)
        return nn(ds, queries), nn(low, dout)

    def dit_early(k):
        def body(q_at, k_at, v_at):
            dk, dv = dit_block(2, q_at, k_at, v_at)
            for at, d in ((q_at, dk), (k_at, dv)):
                sums[:256, at] = jnp.zeros((256, 128), f32)
                sums[256:, at] = d
        heads(k, body)

    flights = {}

    def dit_late(k):
        def body(q_at, k_at, v_at):
            for i in (0, 1):
                _, k0, n = DIT_BLOCKS[i]
                dk, dv = dit_block(i, q_at, k_at, v_at)
                sums[k0:k0 + n, q_at] += dk
                sums[k0:k0 + n, k_at] += dv
            for at, to in ((q_at, k_at), (k_at, v_at)):
                hout[:, at] = sums[:192, at].astype(bf)
                dact[:192, to] = sums[192:384, at].astype(bf)
        heads(k, body)
        flights[k] = [sems.copy(me, "previous", hout.at[:, c], hin.at[:, c]) for c in (pl.ds(256 * k, 256), pl.ds(1024 + 256 * k, 256))]
        for m in flights[k]:
            m.start()

    def settle(k):
        for m in flights[k]:
            m.wait_recv()
        for first in (256 * k, 1024 + 256 * k):
            c = pl.ds(first, 256)
            dact[192:, pl.ds(1024 + first, 256)] = (sums[384:, c] + hin[:, c].astype(f32)).astype(bf)

    def mixed_back(grad, weight, out):
        @chunks(4, 256)
        def _(c):
            out[:, c] = (nt(grad[...], weight[c, :]) * live[...]).astype(bf)

    def add_mixed(base, mix, weight, out):
        @chunks(4, 256)
        def _(c):
            out[:, c] = (base[:, c].astype(f32) + nn(mix[...], weight[:, c])).astype(bf)

    def normed_back():
        @chunks(4, 256)
        def _(c):
            dn[:, c] = nt(dact[...], w2[c, :])

    def hidden_back():
        @chunks(6, 64)
        def _(r):
            dh[r, :] = (cot[r, :].astype(f32) + norm_backward(hidden[r, :].astype(f32), inv1[r, :], dn[r, :])).astype(bf)

    def biases():
        for i, (r0, k0, n) in enumerate(UP_BLOCKS):
            bias1[i, :n] = spans.bias(r0, k0, n, 0, 1)
        for i, (r0, k0, n) in enumerate(DIT_BLOCKS):
            bias2[i, :n] = spans.bias(r0, k0 - 192, n, -2, 0)
        live[...] = (spans.at(0, 384, 0) < spans.length).astype(f32)

    fetch(0)
    line.work(lambda: normalize(x0, n0, inv0), 1.5)
    line.work(biases, 0.7)
    line.work(lambda: turn(n0, n0t), 0.8)
    line.until(parts[0], 1)
    fetch(1)
    fetch(2)
    have(0)
    fetch(3)
    keep = pltpu.make_async_copy(w1, w1_out, local.at[4])
    keep.start()
    line.work(lambda: project(n0, w1, act1, 2, 6), 2.0)
    give1 = sems.copy(me, "previous", act1.at[pl.ds(0, 128), pl.ds(1024, 2048)], halo1)
    give1.start()
    line.work(lambda: project(n0, w1, act1, 0, 2), 1.0)
    for k in range(4):
        line.work(lambda: up_early(k), 1.5)
    give1.wait_recv()
    for k in range(4):
        line.work(lambda: up_late(k), 0.9)
    have(1)
    line.work(lambda: add_mixed(x0, mix1, p1, hidden), 1.0)
    line.work(lambda: normalize(hidden, n1, inv1), 1.2)
    have(2)
    line.work(lambda: project(n1, w2, act2, 2, 6), 2.0)
    give2 = sems.copy(me, "next", act2.at[pl.ds(192, 192), pl.ds(1024, 2048)], halo2)
    give2.start()
    line.work(lambda: project(n1, w2, act2, 0, 2), 1.0)
    have(3)
    line.work(lambda: mixed_back(cot, p2, dmix2), 1.0)
    line.drain()
    for k in range(4):
        dit_early(k)
    turn(n1, n1t)
    give2.wait_recv()
    for k in range(4):
        dit_late(k)
        if k:
            settle(k - 1)
    add_mixed(hidden, mix2, p2, result)
    settle(3)
    normed_back()
    hidden_back()
    mixed_back(dh, p1, dmix1)
    keep.wait()
    for m in [give1, give2] + [m for made in flights.values() for m in made]:
        m.wait_send()


def first_part(*args):
    bf, f32 = jnp.bfloat16, jnp.float32
    v, h = pl.BlockSpec(memory_space=pltpu.VMEM), pl.BlockSpec(memory_space=pl.ANY)
    s = lambda shape, dt=bf: pltpu.VMEM(shape, dt)
    o = lambda *shape, dt=bf: jax.ShapeDtypeStruct(shape, dt)
    scratch = [s((1024, 3072)), s((1024, 1024)), s((1024, 3072)), s((1024, 1024)), s((384, 1024)), s((384, 1024)), s((384, 1), f32),
               s((384, 1024)), s((384, 3072)), s((192, 2048)), s((384, 1024)), s((384, 1024), f32), s((576, 2048), f32),
               s((192, 2048)), s((192, 2048)), s((3, 384, 128), f32), s((3, 384, 128), f32), s((384, 1), f32),
               pltpu.SemaphoreType.DMA((400,)), pltpu.SemaphoreType.DMA((400,)), pltpu.SemaphoreType.DMA((5,))]
    return pl.pallas_call(
        first_kernel,
        out_shape=[o(384, 3072), o(128, 2048), o(1024, 384), o(384, 1, dt=f32), o(1024, 384), o(384, 3072)] + [o(384, 1024)] * 5 + [o(1024, 3072)],
        in_specs=[v] * 2 + [h] * 4 + [pl.BlockSpec(memory_space=pltpu.SMEM)] * 2, out_specs=[v] * 11 + [h], scratch_shapes=scratch,
        compiler_params=pltpu.CompilerParams(collective_id=1, has_side_effects=True, vmem_limit_bytes=60 << 20),
        name="first_part",
    )(*args)


def last_kernel(gp2, gw2, gp1, act, halo, dm, dh, x0, inv, n0t, w1, length, size,
                dframes, t1, tp1, t2, tp2,
                acc1, accp1, acc2, accp2, in1, inp1, in2, inp2, co1, cop1, co2, cop2,
                outbox, kx, vx, bias, dkx, dvx, edge, hout, hin, dact, dcat, dn, send, recv, local):
    me = Place()
    spans = Spans(me, length, size)
    bf = jnp.bfloat16
    sems = Sems(send, recv)
    loads = []
    for i, (t, acc) in enumerate(((gp2, accp2), (gw2, acc2), (gp1, accp1))):
        half = t.shape[1] // 2
        cp = pltpu.make_async_copy(t.at[:, pl.ds(pl.multiple_of(me.c * half, 128), half)], acc, local.at[i])
        cp.start()
        loads.append(cp)
    for i, (r0, k0, n) in enumerate(UP_BLOCKS):
        bias[i, :n] = spans.bias(r0, k0, n, 0, 1)
    greet(me, "next", "previous")
    line = Timeline()
    for i, (t, acc, box, core, gat) in enumerate(((gp2, accp2, inp2, cop2, tp2), (gw2, acc2, in2, co2, t2), (gp1, accp1, inp1, cop1, tp1))):
        for part in reduce_parts(me, sems, t, acc, box, core, gat, loads[i].wait):
            line.launch(part)

    flights = {}

    def attend(g0):
        @pl.loop(g0, g0 + 1)
        def _(g):
            at = pl.multiple_of(g * 128, 128)
            q_at, k_at, v_at = pl.ds(at, 128), pl.ds(at + 1024, 128), pl.ds(at + 2048, 128)
            kx[:384], kx[384:] = act[:, k_at], halo[:, q_at]
            vx[:384], vx[384:] = act[:, v_at], halo[:, k_at]
            dkx[...] = jnp.zeros_like(dkx)
            dvx[...] = jnp.zeros_like(dvx)
            for i, (r0, k0, n) in enumerate(UP_BLOCKS):
                keys, values = kx[k0:k0 + n], vx[k0:k0 + n]
                queries = heads_apart(act[r0:r0 + 128, q_at] * jnp.bfloat16(0.125))
                p = prob_of(keys, queries, bias[i, :n])
                dout = heads_apart(dm[r0:r0 + 128, q_at])
                dp = nt(values, dout)
                ds = (p * (dp - jnp.sum(p * dp, axis=0, keepdims=True))).astype(bf)
                dvx[k0:k0 + n] += nn(p.astype(bf), dout)
                dkx[k0:k0 + n] += nn(ds, queries)
                dact[r0:r0 + 128, q_at] = (heads_together(tn(keys, ds)) * 0.125).astype(bf)
            for full, c_at, e_at in ((dkx, k_at, q_at), (dvx, v_at, k_at)):
                edge[:, e_at] = full[:128]
                dact[128:, c_at] = full[128:384].astype(bf)
                hout[:, e_at] = full[384:].astype(bf)

        if g0 % 2 == 0:
            return
        k = g0 // 2
        made = []
        for first in (0, 1024):
            c = pl.ds(first + 256 * k, 256)
            made.append(sems.copy(me, "next", hout.at[:, c], hin.at[:, c]))
        for m in made:
            m.start()
        flights[k] = made

    def settle(k):
        for m in flights[k]:
            m.wait_recv()
        for first in (0, 1024):
            c = pl.ds(first + 256 * k, 256)
            dact[:128, pl.ds(1024 + first + 256 * k, 256)] = (edge[:, c] + hin[:, c].astype(jnp.float32)).astype(bf)
        for which in range(3):
            mine = pl.ds(pl.multiple_of(which * 1024 + (2 * k + me.c) * 128, 128), 128)
            his = pl.ds(pl.multiple_of(which * 1024 + (2 * k + 1 - me.c) * 128, 128), 128)
            dcat[:, which * 128:which * 128 + 128] = dact[:, mine]
            dcat[:, 384 + which * 128:512 + which * 128] = dact[:, his]

        @pl.loop(0, 4)
        def _(i):
            r = pl.ds(pl.multiple_of(i * 256, 256), 256)
            t = nn(n0t[r, :], dcat[...]).astype(bf)
            acc1[r, k * 384:k * 384 + 384] = t[:, :384]
            outbox[r, k * 384:k * 384 + 384] = t[:, 384:]

    def send_terms(k):
        for which in range(3):
            at = k * 384 + which * 128
            line.launch(Reduce(me, sems, outbox.at[:, pl.ds(at, 128)], acc1, in1, co1, t1, 128, at,
                               which * 1024 + (2 * k + me.c) * 128, rotated(which + 3 * (k % 2))))

    def back_to_normed(i0):
        @pl.loop(i0, i0 + 1)
        def _(i):
            r = pl.ds(pl.multiple_of(i * 256, 256), 256)
            dn[:, r] = nt(dact[...], w1[r, :])

    def back_to_frames():
        @pl.loop(0, 6)
        def _(i):
            r = pl.ds(pl.multiple_of(i * 64, 64), 64)
            x = x0[r, :].astype(jnp.float32)
            inverse = inv[r, :]
            dframes[r, :] = (dh[r, :].astype(jnp.float32) + norm_backward(x, inverse, dn[r, :])).astype(bf)

    line.work(lambda: attend(0), 2.0)
    line.work(lambda: attend(1), 2.0)
    for k in range(1, 4):
        line.work(lambda: attend(2 * k), 2.0)
        line.work(lambda: attend(2 * k + 1), 2.0)
        line.work(lambda: settle(k - 1), 1.2)
        send_terms(k - 1)
    line.work(lambda: settle(3), 1.2)
    send_terms(3)
    for i in range(4):
        line.work(lambda: back_to_normed(i), 1.0)
    line.work(back_to_frames, 1.0)
    line.drain()
    for made in flights.values():
        for m in made:
            m.wait_send()


def last_part(*args):
    bf, f32 = jnp.bfloat16, jnp.float32
    v, h = pl.BlockSpec(memory_space=pltpu.VMEM), pl.BlockSpec(memory_space=pl.ANY)
    s = lambda shape, dt=bf: pltpu.VMEM(shape, dt)
    sizes = (3072, 1024, 3072, 1024)
    scratch = [s((1024, c // 2)) for _ in range(3) for c in sizes]
    scratch += [s((1024, 1536)), s((512, 128)), s((512, 128)), s((3, 384, 128), f32), s((512, 128), f32), s((512, 128), f32),
                s((128, 2048), f32), s((128, 2048)), s((128, 2048)), s((384, 3072)), s((384, 768)), s((384, 1024), f32),
                pltpu.SemaphoreType.DMA((520,)), pltpu.SemaphoreType.DMA((520,)), pltpu.SemaphoreType.DMA((3,))]
    return pl.pallas_call(
        last_kernel,
        out_shape=[jax.ShapeDtypeStruct((384, 1024), bf)] + [jax.ShapeDtypeStruct((256, c), bf) for c in sizes],
        in_specs=[h] * 3 + [v] * 8 + [pl.BlockSpec(memory_space=pltpu.SMEM)] * 2, out_specs=[v] * 5, scratch_shapes=scratch,
        compiler_params=pltpu.CompilerParams(collective_id=2, has_side_effects=True, vmem_limit_bytes=60 << 20),
        name="last_part",
    )(*args)


EPS = 1e-06
DEAD = 1 << 20


def normalize_rows(xfull):
    inverse = lax.rsqrt(jnp.mean(xfull * xfull, axis=-1, keepdims=True) + EPS)
    return (xfull * inverse, inverse)


def norm_backward(xfull, inverse, d_normed):
    row_inner = jnp.mean(d_normed * xfull, axis=-1, keepdims=True)
    return inverse * d_normed - xfull * (inverse * inverse * inverse) * row_inner


def term(left, right):
    return lax.dot_general(left, right, (((0,), (0,)), ((), ())), preferred_element_type=jnp.float32).astype(jnp.bfloat16)


def local(frames, valid_length, span_frames, w1_shard, p1_shard, w2_shard, p2_shard, cotangent):
    bf, f32 = jnp.bfloat16, jnp.float32
    x0, cot = frames[0], cotangent[0]
    act1, halo1, n0t, inv0, n1t, dact2, mix1, mix2, result, dhidden, dmix1, w1 = first_part(
        x0, cot, w1_shard, p1_shard, w2_shard, p2_shard, valid_length, span_frames)
    gp2 = term(mix2, cot)
    gw2 = nn(n1t, dact2).astype(bf)
    gp1 = term(mix1, dhidden)
    scale = float(8 * 6144) ** -0.5
    dframes, *totals = last_part(gp2, gw2, gp1, act1, halo1, dmix1, dhidden, x0, inv0, n0t, w1, valid_length, span_frames)
    return (result[None], dframes[None], *(t.astype(f32) * scale for t in totals))


def solution(mesh):
    rows3, row, flat = P(("fsdp", "dp"), "seq", None), P("fsdp", None), P(("fsdp", "dp"))
    return jax.shard_map(
        local, mesh=mesh, in_specs=(rows3, flat, flat, row, row, row, row, rows3),
        out_specs=(rows3, rows3, row, row, row, row), check_vma=False)
```

```python
import functools
import heapq
import jax
import jax.numpy as jnp
from jax import lax
from jax.experimental import pallas as pl
from jax.experimental.pallas import tpu as pltpu
from jax.sharding import PartitionSpec as P

LINKS = ("xA", "yB", "zA", "xB", "yA", "zB")
PLANE = ("xA", "zA", "xB", "zB")


class Place:
    def __init__(self):
        seq = lax.axis_index("seq")
        self.seq = seq
        self.y = lax.axis_index("fsdp")
        self.zl = lax.axis_index("dp")
        self.x = seq // 4
        self.zh = (seq // 2) % 2
        self.c = seq % 2
        self.z = self.zh * 2 + self.zl

    def bit(self, link):
        p = {"x": self.x, "y": self.y, "z": self.z}[link[0]]
        return ((p + 1) // 2) % 2 if link[1] == "A" else p // 2

    def peer(self, link):
        x, y, z, c = self.x, self.y, self.z, self.c
        if link == "core":
            c = 1 - c
        elif link in ("next", "previous"):
            pass
        elif link[0] == "x":
            x = 3 - x if link[1] == "B" else x + 1 - 2 * (x % 2)
        elif link[0] == "y":
            y = 3 - y if link[1] == "B" else y + 1 - 2 * (y % 2)
        else:
            z = 3 - z if link[1] == "B" else z + 1 - 2 * (z % 2)
        if link == "next":
            return {"seq": (self.seq + 1) % 16, "fsdp": y, "dp": self.zl}
        if link == "previous":
            return {"seq": (self.seq + 15) % 16, "fsdp": y, "dp": self.zl}
        return {"seq": x * 4 + (z // 2) * 2 + c, "fsdp": y, "dp": z % 2}


def greet(me, *more):
    barrier = pltpu.get_barrier_semaphore()
    for link in LINKS + ("core",) + more:
        pl.semaphore_signal(barrier, inc=1, device_id=me.peer(link), device_id_type=pl.DeviceIdType.MESH)
    pl.semaphore_wait(barrier, 7 + len(more))


class Sems:
    def __init__(self, send, recv):
        self.send, self.recv, self.n = send, recv, 0

    def copy(self, me, link, src, dst):
        k = self.n
        self.n += 1
        return pltpu.make_async_remote_copy(
            src_ref=src, dst_ref=dst, send_sem=self.send.at[k], recv_sem=self.recv.at[k],
            device_id=me.peer(link), device_id_type=pl.DeviceIdType.MESH)


def rows(block, off, count):
    return pl.ds(pl.multiple_of(block * 256 + off, 16), count)


class Gather:
    def __init__(self, me, sems, shard, full, width, at, order):
        self.me, self.sems, self.shard, self.full, self.order = me, sems, shard, full, order
        self.cols = pl.ds(pl.multiple_of(at, 128), width)
        self.width = width
        self.sent = []
        y = me.y
        self.a, self.b = y + 1 - 2 * (y % 2), 3 - y
        self.ab = 3 - self.a
        self.steps = len(order) + 1
        self.span = 256 >> (len(order) - 2)
        self.off = 0
        for k, link in enumerate(order[2:]):
            self.off = self.off + me.bit(link) * (self.span << k)
        self.wait_for = []

    def own(self):
        return self.shard.at[pl.ds(pl.multiple_of(self.off + 0, 16), self.span), self.cols]

    def blk(self, block):
        return self.full.at[rows(block, self.off, self.span), self.cols]

    def _go(self, link, pairs):
        made = [self.sems.copy(self.me, link, s, d) for s, d in pairs]
        for m in made:
            m.start()
        self.sent += made
        self.wait_for = made

    def start(self, step):
        me = self.me
        if step < 2:
            link = self.order[step]
            pairs = [(self.own(), self.blk(me.y))]
            if step == 1:
                other = self.a if self.order[0] == "yA" else self.b
                pairs.append((self.blk(other), self.blk(other)))
            self._go(link, pairs)
        elif step < len(self.order):
            self._go(self.order[step], [(self.blk(k), self.blk(k)) for k in (self.a, self.b, self.ab)])
        else:
            self._go("core", [(self.blk(k), self.blk(k)) for k in (self.a, self.b, self.ab)])

    def load(self, step):
        blocks = 1 if step == 0 else 2 if step == 1 else 3
        return (self.order + ("core",))[step], blocks * self.span * self.width * 2, 0.0

    def finish(self, step):
        for m in self.wait_for:
            m.wait_recv()
        if 2 <= step < len(self.order):
            link = self.order[step]
            self.off = self.off - self.me.bit(link) * self.span
            self.span *= 2

    def close(self):
        for m in self.sent:
            m.wait_send()


class Reduce:
    def __init__(self, me, sems, source, acc, inbox, inbox_core, gat, width, at, gat_at, order, ready=None):
        self.me, self.sems, self.source, self.acc, self.inbox, self.inbox_core, self.gat = me, sems, source, acc, inbox, inbox_core, gat
        self.width, self.order, self.ready = width, order, ready
        self.back = tuple(l for l in reversed(order) if l[0] != "y")
        self.cols = pl.ds(at, width)
        self.mine = pl.ds(pl.multiple_of(gat_at, 128), width)
        self.sent = []
        y = me.y
        a, b = y + 1 - 2 * (y % 2), 3 - y
        self.y, self.a, self.b, self.ab = y, a, b, 3 - a
        self.live = None
        self.off, self.span, self.inbox_at = 0, 256, 0
        self.steps = 12
        self.left = 1024

    def _go(self, link, pairs):
        made = [self.sems.copy(self.me, link, s, d) for s, d in pairs]
        for m in made:
            m.start()
        self.sent += made
        self.wait_for = made

    def load(self, step):
        line = 2 * self.width
        if step == 0:
            return "core", 1024 * line, 1024 * line / 1.5e6
        if step <= 6:
            return self.order[step - 1], (512 >> (step - 1)) * line, (512 >> (step - 1)) * line / 1.5e6 + 0.1
        if step <= 10:
            return self.back[step - 7], (16 << (step - 7)) * line, 0.0
        return "core", 256 * line, 0.0

    def start(self, step):
        me = self.me
        if step == 0:
            self._go("core", [(self.source, self.inbox_core.at[:, self.cols])])
        elif step <= 6:
            link = self.order[step - 1]
            bit = me.bit(link)
            if link[0] == "y":
                y, a, b, ab = self.y, self.a, self.b, self.ab
                if self.live is None:
                    keep, send = ([y, b], [a, ab]) if link[1] == "A" else ([y, a], [b, ab])
                else:
                    keep, send = [y], [a if link[1] == "A" else b]
                self.live = keep
                keep_off = send_off = self.off
            else:
                self.span //= 2
                keep = send = [0, 1, 2, 3] if self.live is None else self.live
                keep_off = self.off + bit * self.span
                send_off = self.off + (1 - bit) * self.span
                self.off = keep_off
            pairs, self.adds = [], []
            for k, s in zip(keep, send, strict=True):
                box = pl.ds(self.inbox_at, self.span)
                pairs.append((self.acc.at[rows(s, send_off, self.span), self.cols], self.inbox.at[box, self.cols]))
                self.adds.append((k * 256 + keep_off, self.inbox_at, self.span))
                self.inbox_at += self.span
            self._go(link, pairs)
        elif step <= 10:
            here = self.gat.at[pl.ds(pl.multiple_of(self.off, 16), self.span), self.mine]
            self._go(self.back[step - 7], [(here, here)])
        else:
            here = self.gat.at[:, self.mine]
            self._go("core", [(here, here)])

    def finish(self, step):
        for m in self.wait_for:
            m.wait_recv()
        if step == 0:
            if self.ready is not None:
                self.ready()

            @pl.loop(0, 1024 // 64)
            def _(i):
                r = pl.ds(pl.multiple_of(i * 64, 64), 64)
                self.acc[r, self.cols] = self.acc[r, self.cols] + self.inbox_core[r, self.cols]
        elif step <= 6:
            for at, box, count in self.adds:
                chunk = min(count, 64)

                @pl.loop(0, count // chunk)
                def _(i):
                    r = pl.ds(pl.multiple_of(at + i * chunk, 16), chunk)
                    q = pl.ds(pl.multiple_of(box + i * chunk, 16), chunk)
                    self.acc[r, self.cols] = self.acc[r, self.cols] + self.inbox[q, self.cols]
            if step == 6:
                self.gat[pl.ds(pl.multiple_of(self.off, 16), self.span), self.mine] = self.acc[
                    rows(self.y, self.off, self.span), self.cols]
        elif step <= 10:
            self.off = self.off - self.me.bit(self.back[step - 7]) * self.span
            self.span *= 2

    def close(self):
        for m in self.sent:
            m.wait_send()


class Timeline:
    def __init__(self):
        self.now, self.free, self.queue, self.count, self.parts = 0.0, {}, [], 0, []

    def launch(self, part, step=0):
        if step == 0:
            self.parts.append(part)
            part.over, part.past = False, -1
        link, size, cost = part.load(step)
        part.start(step)
        begin = max(self.now, self.free.get(link, 0.0))
        end = begin + size / (0.45e6 if link == "core" else 0.036e6)
        self.free[link] = end
        heapq.heappush(self.queue, (end + (1.5 if link == "core" else 3.0), self.count, part, step, cost))
        self.count += 1

    def _one(self):
        end, _, part, step, cost = heapq.heappop(self.queue)
        self.now = max(self.now, end)
        part.finish(step)
        part.over, part.past = step + 1 == part.steps, step
        self.now += cost
        if step + 1 < part.steps:
            self.launch(part, step + 1)

    def poll(self):
        while self.queue and self.queue[0][0] <= self.now:
            self._one()

    def work(self, what, time):
        what()
        self.now += time
        self.poll()

    def until(self, parts, step=9):
        while any(not p.over and p.past < step for p in parts):
            self._one()

    def drain(self):
        while self.queue:
            self._one()
        for part in self.parts:
            part.close()


def rotated(i):
    return tuple(LINKS[(i + j) % 6] for j in range(6))


def reduce_parts(me, sems, terms, acc, inbox, inbox_core, gat, ready):
    columns = terms.shape[1]
    half = columns // 2
    n, starts = (6, (0, 1, 2, 3, 4, 5)) if columns == 3072 else (4, (0, 1, 3, 4))
    width = half // n
    out = []
    for i in range(n):
        source = terms.at[:, pl.ds(pl.multiple_of((1 - me.c) * half + i * width, 128), width)]
        out.append(Reduce(me, sems, source, acc, inbox, inbox_core, gat, width, i * width, me.c * half + i * width,
                          rotated(starts[i]), ready if i == 0 else None))
    return out


def gather_parts(me, sems, shard, full):
    half = full.shape[1] // 2
    width = half // 4
    orders = (("yA", "yB", "xA", "xB"), ("yB", "yA", "zA", "zB"), ("yA", "yB", "xB", "xA"), ("yB", "yA", "zB", "zA"))
    return [Gather(me, sems, shard, full, width, me.c * half + i * width, order) for i, order in enumerate(orders)]


FAR = -1e30


def heads_apart(block):
    first = lax.broadcasted_iota(jnp.int32, block.shape, 1) < 64
    zero = jnp.zeros_like(block)
    return jnp.concatenate([jnp.where(first, block, zero), jnp.where(first, zero, block)], axis=0)


def heads_together(wide):
    count = wide.shape[1] // 2
    return jnp.concatenate([wide[:64, :count], wide[64:, count:]], axis=0).T


def nt(a, b):
    return lax.dot_general(a, b, (((1,), (1,)), ((), ())), preferred_element_type=jnp.float32)


def tn(a, b):
    return lax.dot_general(a, b, (((0,), (0,)), ((), ())), preferred_element_type=jnp.float32)


def nn(a, b):
    return jnp.dot(a, b, preferred_element_type=jnp.float32)


def window_bias(key_span, query_span, low, high):
    gap = key_span - query_span
    return jnp.where((gap >= low) & (gap <= high), 0.0, FAR).astype(jnp.float32)


def prob_of(keys, queries, bias):
    score = nt(keys, queries) + jnp.concatenate([bias, bias], axis=1)
    terms = jnp.exp(score - jnp.max(score, axis=0, keepdims=True))
    return terms * (1.0 / jnp.sum(terms, axis=0, keepdims=True))


class Spans:
    def __init__(self, me, length, size):
        self.first, self.length = me.seq * 384, length[0]
        self.inverse = 1.0 / jnp.full((1, 1), size[0].astype(jnp.float32))

    def at(self, start, count, axis):
        shape = (count, 1) if axis == 0 else (1, count)
        return self.first + start + lax.broadcasted_iota(jnp.int32, shape, axis)

    def number(self, frames):
        return jnp.floor((frames.astype(jnp.float32) + 0.5) * self.inverse)

    def bias(self, query, key, count, low, high):
        frames = self.at(key, count, 0)
        alive = (frames >= 0) & (frames < self.length)
        return window_bias(jnp.where(alive, self.number(frames), 1e6), self.number(self.at(query, 128, 1)), low, high)


UP_BLOCKS = ((0, 0, 256), (128, 64, 320), (256, 192, 320))
DIT_BLOCKS = ((0, 0, 384), (128, 128, 384), (256, 256, 320))


def first_kernel(x0, cot, s0, s1, s2, s3, length, size,
                 act1, halo1, n0t, inv0, n1t, dact, mix1, mix2, result, dh, dmix1, w1_out,
                 w1, p1, w2, p2, n0, n1, inv1, hidden, act2, halo2, dmix2, dn, sums, hout, hin, bias1, bias2, live, send, recv, local):
    me = Place()
    spans = Spans(me, length, size)
    bf, f32 = jnp.bfloat16, jnp.float32
    sems = Sems(send, recv)
    shards, fulls = (s0, s1, s2, s3), (w1, p1, w2, p2)
    own = [pltpu.make_async_copy(s, f.at[rows(me.y, 0, 256), :], local.at[i]) for i, (s, f) in enumerate(zip(shards, fulls, strict=True))]
    for cp in own:
        cp.start()
    greet(me, "next", "previous")
    line = Timeline()
    parts = [gather_parts(me, sems, s, f) for s, f in zip(shards, fulls, strict=True)]

    def fetch(i):
        for part in parts[i]:
            line.launch(part)

    def have(i):
        line.until(parts[i])
        own[i].wait()

    def chunks(count, width):
        def run(body):
            @pl.loop(0, count)
            def _(i):
                body(pl.ds(pl.multiple_of(i * width, width), width))
        return run

    def normalize(source, normed, inverse):
        @chunks(6, 64)
        def _(r):
            value, inv = normalize_rows(source[r, :].astype(f32))
            normed[r, :] = value.astype(bf)
            inverse[r, :] = inv

    def turn(normed, turned):
        @chunks(4, 256)
        def _(c):
            turned[c, :] = normed[:, c].T

    def project(normed, weight, act, low, high):
        @pl.loop(low, high)
        def _(i):
            c = pl.ds(pl.multiple_of(i * 512, 512), 512)
            act[:, c] = nn(normed[...], weight[:, c]).astype(bf)

    def heads(k, body):
        @pl.loop(2 * k, 2 * k + 2)
        def _(g):
            at = pl.multiple_of(g * 128, 128)
            body(pl.ds(at, 128), pl.ds(at + 1024, 128), pl.ds(at + 2048, 128))

    def up_block(i, q_at, k_at, v_at):
        r0, k0, n = UP_BLOCKS[i]
        keys, values = act1[k0:min(k0 + n, 384), k_at], act1[k0:min(k0 + n, 384), v_at]
        if i == 2:
            keys = jnp.concatenate([keys, halo1[:, q_at]], axis=0)
            values = jnp.concatenate([values, halo1[:, k_at]], axis=0)
        queries = heads_apart(act1[r0:r0 + 128, q_at] * jnp.bfloat16(0.125))
        p = prob_of(keys, queries, bias1[i, :n])
        mix1[r0:r0 + 128, q_at] = (heads_together(tn(values, p.astype(bf))) * live[r0:r0 + 128]).astype(bf)

    def up_early(k):
        def body(*at):
            up_block(0, *at)
            up_block(1, *at)
        heads(k, body)

    def up_late(k):
        heads(k, lambda *at: up_block(2, *at))

    def dit_block(i, q_at, k_at, v_at):
        r0, k0, n = DIT_BLOCKS[i]
        keys, values = act2[max(k0 - 192, 0):k0 - 192 + n, k_at], act2[max(k0 - 192, 0):k0 - 192 + n, v_at]
        if k0 < 192:
            keys = jnp.concatenate([halo2[k0:, q_at], keys], axis=0)
            values = jnp.concatenate([halo2[k0:, k_at], values], axis=0)
        queries = heads_apart(act2[r0:r0 + 128, q_at] * jnp.bfloat16(0.125))
        p = prob_of(keys, queries, bias2[i, :n])
        low = p.astype(bf)
        mix2[r0:r0 + 128, q_at] = (heads_together(tn(values, low)) * live[r0:r0 + 128]).astype(bf)
        dout = heads_apart(dmix2[r0:r0 + 128, q_at])
        dp = nt(values, dout)
        ds = (p * (dp - jnp.sum(p * dp, axis=0, keepdims=True))).astype(bf)
        dact[r0:r0 + 128, q_at] = (heads_together(tn(keys, ds)) * 0.125).astype(bf)
        return nn(ds, queries), nn(low, dout)

    def dit_early(k):
        def body(q_at, k_at, v_at):
            dk, dv = dit_block(2, q_at, k_at, v_at)
            for at, d in ((q_at, dk), (k_at, dv)):
                sums[:256, at] = jnp.zeros((256, 128), f32)
                sums[256:, at] = d
        heads(k, body)

    flights = {}

    def dit_late(k):
        def body(q_at, k_at, v_at):
            for i in (0, 1):
                _, k0, n = DIT_BLOCKS[i]
                dk, dv = dit_block(i, q_at, k_at, v_at)
                sums[k0:k0 + n, q_at] += dk
                sums[k0:k0 + n, k_at] += dv
            for at, to in ((q_at, k_at), (k_at, v_at)):
                hout[:, at] = sums[:192, at].astype(bf)
                dact[:192, to] = sums[192:384, at].astype(bf)
        heads(k, body)
        flights[k] = [sems.copy(me, "previous", hout.at[:, c], hin.at[:, c]) for c in (pl.ds(256 * k, 256), pl.ds(1024 + 256 * k, 256))]
        for m in flights[k]:
            m.start()

    def settle(k):
        for m in flights[k]:
            m.wait_recv()
        for first in (256 * k, 1024 + 256 * k):
            c = pl.ds(first, 256)
            dact[192:, pl.ds(1024 + first, 256)] = (sums[384:, c] + hin[:, c].astype(f32)).astype(bf)

    def mixed_back(grad, weight, out):
        @chunks(4, 256)
        def _(c):
            out[:, c] = (nt(grad[...], weight[c, :]) * live[...]).astype(bf)

    def add_mixed(base, mix, weight, out):
        @chunks(4, 256)
        def _(c):
            out[:, c] = (base[:, c].astype(f32) + nn(mix[...], weight[:, c])).astype(bf)

    def normed_back():
        @chunks(4, 256)
        def _(c):
            dn[:, c] = nt(dact[...], w2[c, :])

    def hidden_back():
        @chunks(6, 64)
        def _(r):
            dh[r, :] = (cot[r, :].astype(f32) + norm_backward(hidden[r, :].astype(f32), inv1[r, :], dn[r, :])).astype(bf)

    def biases():
        for i, (r0, k0, n) in enumerate(UP_BLOCKS):
            bias1[i, :n] = spans.bias(r0, k0, n, 0, 1)
        for i, (r0, k0, n) in enumerate(DIT_BLOCKS):
            bias2[i, :n] = spans.bias(r0, k0 - 192, n, -2, 0)
        live[...] = (spans.at(0, 384, 0) < spans.length).astype(f32)

    fetch(0)
    line.work(lambda: normalize(x0, n0, inv0), 1.5)
    line.work(biases, 0.7)
    line.work(lambda: turn(n0, n0t), 0.8)
    line.until(parts[0], 1)
    fetch(1)
    fetch(2)
    have(0)
    fetch(3)
    keep = pltpu.make_async_copy(w1, w1_out, local.at[4])
    keep.start()
    line.work(lambda: project(n0, w1, act1, 2, 6), 2.0)
    give1 = sems.copy(me, "previous", act1.at[pl.ds(0, 128), pl.ds(1024, 2048)], halo1)
    give1.start()
    line.work(lambda: project(n0, w1, act1, 0, 2), 1.0)
    for k in range(4):
        line.work(lambda: up_early(k), 1.5)
    give1.wait_recv()
    for k in range(4):
        line.work(lambda: up_late(k), 0.9)
    have(1)
    line.work(lambda: add_mixed(x0, mix1, p1, hidden), 1.0)
    line.work(lambda: normalize(hidden, n1, inv1), 1.2)
    have(2)
    line.work(lambda: project(n1, w2, act2, 2, 6), 2.0)
    give2 = sems.copy(me, "next", act2.at[pl.ds(192, 192), pl.ds(1024, 2048)], halo2)
    give2.start()
    line.work(lambda: project(n1, w2, act2, 0, 2), 1.0)
    have(3)
    line.work(lambda: mixed_back(cot, p2, dmix2), 1.0)
    line.drain()
    for k in range(4):
        dit_early(k)
    turn(n1, n1t)
    give2.wait_recv()
    for k in range(4):
        dit_late(k)
        if k:
            settle(k - 1)
    add_mixed(hidden, mix2, p2, result)
    settle(3)
    normed_back()
    hidden_back()
    mixed_back(dh, p1, dmix1)
    keep.wait()
    for m in [give1, give2] + [m for made in flights.values() for m in made]:
        m.wait_send()


def first_part(*args):
    bf, f32 = jnp.bfloat16, jnp.float32
    v, h = pl.BlockSpec(memory_space=pltpu.VMEM), pl.BlockSpec(memory_space=pl.ANY)
    s = lambda shape, dt=bf: pltpu.VMEM(shape, dt)
    o = lambda *shape, dt=bf: jax.ShapeDtypeStruct(shape, dt)
    scratch = [s((1024, 3072)), s((1024, 1024)), s((1024, 3072)), s((1024, 1024)), s((384, 1024)), s((384, 1024)), s((384, 1), f32),
               s((384, 1024)), s((384, 3072)), s((192, 2048)), s((384, 1024)), s((384, 1024), f32), s((576, 2048), f32),
               s((192, 2048)), s((192, 2048)), s((3, 384, 128), f32), s((3, 384, 128), f32), s((384, 1), f32),
               pltpu.SemaphoreType.DMA((400,)), pltpu.SemaphoreType.DMA((400,)), pltpu.SemaphoreType.DMA((5,))]
    return pl.pallas_call(
        first_kernel,
        out_shape=[o(384, 3072), o(128, 2048), o(1024, 384), o(384, 1, dt=f32), o(1024, 384), o(384, 3072)] + [o(384, 1024)] * 5 + [o(1024, 3072)],
        in_specs=[v] * 2 + [h] * 4 + [pl.BlockSpec(memory_space=pltpu.SMEM)] * 2, out_specs=[v] * 11 + [h], scratch_shapes=scratch,
        compiler_params=pltpu.CompilerParams(collective_id=1, has_side_effects=True, vmem_limit_bytes=60 << 20),
        name="first_part",
    )(*args)


def last_kernel(gp2, gw2, gp1, act, halo, dm, dh, x0, inv, n0t, w1, length, size,
                dframes, t1, tp1, t2, tp2,
                acc1, accp1, acc2, accp2, in1, inp1, in2, inp2, co1, cop1, co2, cop2,
                outbox, kx, vx, bias, dkx, dvx, edge, hout, hin, dact, dcat, dn, send, recv, local):
    me = Place()
    spans = Spans(me, length, size)
    bf = jnp.bfloat16
    sems = Sems(send, recv)
    loads = []
    for i, (t, acc) in enumerate(((gp2, accp2), (gw2, acc2), (gp1, accp1))):
        half = t.shape[1] // 2
        cp = pltpu.make_async_copy(t.at[:, pl.ds(pl.multiple_of(me.c * half, 128), half)], acc, local.at[i])
        cp.start()
        loads.append(cp)
    for i, (r0, k0, n) in enumerate(UP_BLOCKS):
        bias[i, :n] = spans.bias(r0, k0, n, 0, 1)
    greet(me, "next", "previous")
    line = Timeline()
    for i, (t, acc, box, core, gat) in enumerate(((gp2, accp2, inp2, cop2, tp2), (gw2, acc2, in2, co2, t2), (gp1, accp1, inp1, cop1, tp1))):
        for part in reduce_parts(me, sems, t, acc, box, core, gat, loads[i].wait):
            line.launch(part)

    flights = {}

    def attend(g0):
        @pl.loop(g0, g0 + 1)
        def _(g):
            at = pl.multiple_of(g * 128, 128)
            q_at, k_at, v_at = pl.ds(at, 128), pl.ds(at + 1024, 128), pl.ds(at + 2048, 128)
            kx[:384], kx[384:] = act[:, k_at], halo[:, q_at]
            vx[:384], vx[384:] = act[:, v_at], halo[:, k_at]
            dkx[...] = jnp.zeros_like(dkx)
            dvx[...] = jnp.zeros_like(dvx)
            for i, (r0, k0, n) in enumerate(UP_BLOCKS):
                keys, values = kx[k0:k0 + n], vx[k0:k0 + n]
                queries = heads_apart(act[r0:r0 + 128, q_at] * jnp.bfloat16(0.125))
                p = prob_of(keys, queries, bias[i, :n])
                dout = heads_apart(dm[r0:r0 + 128, q_at])
                dp = nt(values, dout)
                ds = (p * (dp - jnp.sum(p * dp, axis=0, keepdims=True))).astype(bf)
                dvx[k0:k0 + n] += nn(p.astype(bf), dout)
                dkx[k0:k0 + n] += nn(ds, queries)
                dact[r0:r0 + 128, q_at] = (heads_together(tn(keys, ds)) * 0.125).astype(bf)
            for full, c_at, e_at in ((dkx, k_at, q_at), (dvx, v_at, k_at)):
                edge[:, e_at] = full[:128]
                dact[128:, c_at] = full[128:384].astype(bf)
                hout[:, e_at] = full[384:].astype(bf)

        if g0 % 2 == 0:
            return
        k = g0 // 2
        made = []
        for first in (0, 1024):
            c = pl.ds(first + 256 * k, 256)
            made.append(sems.copy(me, "next", hout.at[:, c], hin.at[:, c]))
        for m in made:
            m.start()
        flights[k] = made

    def settle(k):
        for m in flights[k]:
            m.wait_recv()
        for first in (0, 1024):
            c = pl.ds(first + 256 * k, 256)
            dact[:128, pl.ds(1024 + first + 256 * k, 256)] = (edge[:, c] + hin[:, c].astype(jnp.float32)).astype(bf)
        for which in range(3):
            mine = pl.ds(pl.multiple_of(which * 1024 + (2 * k + me.c) * 128, 128), 128)
            his = pl.ds(pl.multiple_of(which * 1024 + (2 * k + 1 - me.c) * 128, 128), 128)
            dcat[:, which * 128:which * 128 + 128] = dact[:, mine]
            dcat[:, 384 + which * 128:512 + which * 128] = dact[:, his]

        @pl.loop(0, 4)
        def _(i):
            r = pl.ds(pl.multiple_of(i * 256, 256), 256)
            t = nn(n0t[r, :], dcat[...]).astype(bf)
            acc1[r, k * 384:k * 384 + 384] = t[:, :384]
            outbox[r, k * 384:k * 384 + 384] = t[:, 384:]

    def send_terms(k):
        for which in range(3):
            at = k * 384 + which * 128
            line.launch(Reduce(me, sems, outbox.at[:, pl.ds(at, 128)], acc1, in1, co1, t1, 128, at,
                               which * 1024 + (2 * k + me.c) * 128, rotated(which + 3 * (k % 2))))

    def back_to_normed(i0):
        @pl.loop(i0, i0 + 1)
        def _(i):
            r = pl.ds(pl.multiple_of(i * 256, 256), 256)
            dn[:, r] = nt(dact[...], w1[r, :])

    def back_to_frames():
        @pl.loop(0, 6)
        def _(i):
            r = pl.ds(pl.multiple_of(i * 64, 64), 64)
            x = x0[r, :].astype(jnp.float32)
            inverse = inv[r, :]
            dframes[r, :] = (dh[r, :].astype(jnp.float32) + norm_backward(x, inverse, dn[r, :])).astype(bf)

    line.work(lambda: attend(0), 2.0)
    line.work(lambda: attend(1), 2.0)
    for k in range(1, 4):
        line.work(lambda: attend(2 * k), 2.0)
        line.work(lambda: attend(2 * k + 1), 2.0)
        line.work(lambda: settle(k - 1), 1.2)
        send_terms(k - 1)
    line.work(lambda: settle(3), 1.2)
    send_terms(3)
    for i in range(4):
        line.work(lambda: back_to_normed(i), 1.0)
    line.work(back_to_frames, 1.0)
    line.drain()
    for made in flights.values():
        for m in made:
            m.wait_send()


def last_part(*args):
    bf, f32 = jnp.bfloat16, jnp.float32
    v, h = pl.BlockSpec(memory_space=pltpu.VMEM), pl.BlockSpec(memory_space=pl.ANY)
    s = lambda shape, dt=bf: pltpu.VMEM(shape, dt)
    sizes = (3072, 1024, 3072, 1024)
    scratch = [s((1024, c // 2)) for _ in range(3) for c in sizes]
    scratch += [s((1024, 1536)), s((512, 128)), s((512, 128)), s((3, 384, 128), f32), s((512, 128), f32), s((512, 128), f32),
                s((128, 2048), f32), s((128, 2048)), s((128, 2048)), s((384, 3072)), s((384, 768)), s((384, 1024), f32),
                pltpu.SemaphoreType.DMA((520,)), pltpu.SemaphoreType.DMA((520,)), pltpu.SemaphoreType.DMA((3,))]
    return pl.pallas_call(
        last_kernel,
        out_shape=[jax.ShapeDtypeStruct((384, 1024), bf)] + [jax.ShapeDtypeStruct((256, c), bf) for c in sizes],
        in_specs=[h] * 3 + [v] * 8 + [pl.BlockSpec(memory_space=pltpu.SMEM)] * 2, out_specs=[v] * 5, scratch_shapes=scratch,
        compiler_params=pltpu.CompilerParams(collective_id=2, has_side_effects=True, vmem_limit_bytes=60 << 20),
        name="last_part",
    )(*args)


EPS = 1e-06
DEAD = 1 << 20


def normalize_rows(xfull):
    inverse = lax.rsqrt(jnp.mean(xfull * xfull, axis=-1, keepdims=True) + EPS)
    return (xfull * inverse, inverse)


def norm_backward(xfull, inverse, d_normed):
    row_inner = jnp.mean(d_normed * xfull, axis=-1, keepdims=True)
    return inverse * d_normed - xfull * (inverse * inverse * inverse) * row_inner


def term(left, right):
    return lax.dot_general(left, right, (((0,), (0,)), ((), ())), preferred_element_type=jnp.float32).astype(jnp.bfloat16)


def local(frames, valid_length, span_frames, w1_shard, p1_shard, w2_shard, p2_shard, cotangent):
    bf, f32 = jnp.bfloat16, jnp.float32
    x0, cot = frames[0], cotangent[0]
    act1, halo1, n0t, inv0, n1t, dact2, mix1, mix2, result, dhidden, dmix1, w1 = first_part(
        x0, cot, w1_shard, p1_shard, w2_shard, p2_shard, valid_length, span_frames)
    gp2 = term(mix2, cot)
    gw2 = nn(n1t, dact2).astype(bf)
    gp1 = term(mix1, dhidden)
    scale = float(8 * 6144) ** -0.5
    dframes, *totals = last_part(gp2, gw2, gp1, act1, halo1, dmix1, dhidden, x0, inv0, n0t, w1, valid_length, span_frames)
    return (result[None], dframes[None], *(t.astype(f32) * scale for t in totals))


def solution(mesh):
    rows3, row, flat = P(("fsdp", "dp"), "seq", None), P("fsdp", None), P(("fsdp", "dp"))
    return jax.shard_map(
        local, mesh=mesh, in_specs=(rows3, flat, flat, row, row, row, row, rows3),
        out_specs=(rows3, rows3, row, row, row, row), check_vma=False)
```

```python
import functools
import heapq
import jax
import jax.numpy as jnp
from jax import lax
from jax.experimental import pallas as pl
from jax.experimental.pallas import tpu as pltpu
from jax.sharding import PartitionSpec as P

LINKS = ("xA", "yB", "zA", "xB", "yA", "zB")
PLANE = ("xA", "zA", "xB", "zB")


class Place:
    def __init__(self):
        seq = lax.axis_index("seq")
        self.seq = seq
        self.y = lax.axis_index("fsdp")
        self.zl = lax.axis_index("dp")
        self.x = seq // 4
        self.zh = (seq // 2) % 2
        self.c = seq % 2
        self.z = self.zh * 2 + self.zl

    def bit(self, link):
        p = {"x": self.x, "y": self.y, "z": self.z}[link[0]]
        return ((p + 1) // 2) % 2 if link[1] == "A" else p // 2

    def peer(self, link):
        x, y, z, c = self.x, self.y, self.z, self.c
        if link == "core":
            c = 1 - c
        elif link in ("next", "previous"):
            pass
        elif link[0] == "x":
            x = 3 - x if link[1] == "B" else x + 1 - 2 * (x % 2)
        elif link[0] == "y":
            y = 3 - y if link[1] == "B" else y + 1 - 2 * (y % 2)
        else:
            z = 3 - z if link[1] == "B" else z + 1 - 2 * (z % 2)
        if link == "next":
            return {"seq": (self.seq + 1) % 16, "fsdp": y, "dp": self.zl}
        if link == "previous":
            return {"seq": (self.seq + 15) % 16, "fsdp": y, "dp": self.zl}
        return {"seq": x * 4 + (z // 2) * 2 + c, "fsdp": y, "dp": z % 2}


def greet(me, *more):
    barrier = pltpu.get_barrier_semaphore()
    for link in LINKS + ("core",) + more:
        pl.semaphore_signal(barrier, inc=1, device_id=me.peer(link), device_id_type=pl.DeviceIdType.MESH)
    pl.semaphore_wait(barrier, 7 + len(more))


class Sems:
    def __init__(self, send, recv):
        self.send, self.recv, self.n = send, recv, 0

    def copy(self, me, link, src, dst):
        k = self.n
        self.n += 1
        return pltpu.make_async_remote_copy(
            src_ref=src, dst_ref=dst, send_sem=self.send.at[k], recv_sem=self.recv.at[k],
            device_id=me.peer(link), device_id_type=pl.DeviceIdType.MESH)


def rows(block, off, count):
    return pl.ds(pl.multiple_of(block * 256 + off, 16), count)


class Gather:
    def __init__(self, me, sems, shard, full, width, at, order):
        self.me, self.sems, self.shard, self.full, self.order = me, sems, shard, full, order
        self.cols = pl.ds(pl.multiple_of(at, 128), width)
        self.width = width
        self.sent = []
        y = me.y
        self.a, self.b = y + 1 - 2 * (y % 2), 3 - y
        self.ab = 3 - self.a
        self.steps = len(order) + 1
        self.span = 256 >> (len(order) - 2)
        self.off = 0
        for k, link in enumerate(order[2:]):
            self.off = self.off + me.bit(link) * (self.span << k)
        self.wait_for = []

    def own(self):
        return self.shard.at[pl.ds(pl.multiple_of(self.off + 0, 16), self.span), self.cols]

    def blk(self, block):
        return self.full.at[rows(block, self.off, self.span), self.cols]

    def _go(self, link, pairs):
        made = [self.sems.copy(self.me, link, s, d) for s, d in pairs]
        for m in made:
            m.start()
        self.sent += made
        self.wait_for = made

    def start(self, step):
        me = self.me
        if step < 2:
            link = self.order[step]
            pairs = [(self.own(), self.blk(me.y))]
            if step == 1:
                other = self.a if self.order[0] == "yA" else self.b
                pairs.append((self.blk(other), self.blk(other)))
            self._go(link, pairs)
        elif step < len(self.order):
            self._go(self.order[step], [(self.blk(k), self.blk(k)) for k in (self.a, self.b, self.ab)])
        else:
            self._go("core", [(self.blk(k), self.blk(k)) for k in (self.a, self.b, self.ab)])

    def load(self, step):
        blocks = 1 if step == 0 else 2 if step == 1 else 3
        return (self.order + ("core",))[step], blocks * self.span * self.width * 2, 0.0

    def finish(self, step):
        for m in self.wait_for:
            m.wait_recv()
        if 2 <= step < len(self.order):
            link = self.order[step]
            self.off = self.off - self.me.bit(link) * self.span
            self.span *= 2

    def close(self):
        for m in self.sent:
            m.wait_send()


class Reduce:
    def __init__(self, me, sems, source, acc, inbox, inbox_core, gat, width, at, gat_at, order, ready=None):
        self.me, self.sems, self.source, self.acc, self.inbox, self.inbox_core, self.gat = me, sems, source, acc, inbox, inbox_core, gat
        self.width, self.order, self.ready = width, order, ready
        self.back = tuple(l for l in reversed(order) if l[0] != "y")
        self.cols = pl.ds(at, width)
        self.mine = pl.ds(pl.multiple_of(gat_at, 128), width)
        self.sent = []
        y = me.y
        a, b = y + 1 - 2 * (y % 2), 3 - y
        self.y, self.a, self.b, self.ab = y, a, b, 3 - a
        self.live = None
        self.off, self.span, self.inbox_at = 0, 256, 0
        self.steps = 12
        self.left = 1024

    def _go(self, link, pairs):
        made = [self.sems.copy(self.me, link, s, d) for s, d in pairs]
        for m in made:
            m.start()
        self.sent += made
        self.wait_for = made

    def load(self, step):
        line = 2 * self.width
        if step == 0:
            return "core", 1024 * line, 1024 * line / 1.5e6
        if step <= 6:
            return self.order[step - 1], (512 >> (step - 1)) * line, (512 >> (step - 1)) * line / 1.5e6 + 0.1
        if step <= 10:
            return self.back[step - 7], (16 << (step - 7)) * line, 0.0
        return "core", 256 * line, 0.0

    def start(self, step):
        me = self.me
        if step == 0:
            self._go("core", [(self.source, self.inbox_core.at[:, self.cols])])
        elif step <= 6:
            link = self.order[step - 1]
            bit = me.bit(link)
            if link[0] == "y":
                y, a, b, ab = self.y, self.a, self.b, self.ab
                if self.live is None:
                    keep, send = ([y, b], [a, ab]) if link[1] == "A" else ([y, a], [b, ab])
                else:
                    keep, send = [y], [a if link[1] == "A" else b]
                self.live = keep
                keep_off = send_off = self.off
            else:
                self.span //= 2
                keep = send = [0, 1, 2, 3] if self.live is None else self.live
                keep_off = self.off + bit * self.span
                send_off = self.off + (1 - bit) * self.span
                self.off = keep_off
            pairs, self.adds = [], []
            for k, s in zip(keep, send, strict=True):
                box = pl.ds(self.inbox_at, self.span)
                pairs.append((self.acc.at[rows(s, send_off, self.span), self.cols], self.inbox.at[box, self.cols]))
                self.adds.append((k * 256 + keep_off, self.inbox_at, self.span))
                self.inbox_at += self.span
            self._go(link, pairs)
        elif step <= 10:
            here = self.gat.at[pl.ds(pl.multiple_of(self.off, 16), self.span), self.mine]
            self._go(self.back[step - 7], [(here, here)])
        else:
            here = self.gat.at[:, self.mine]
            self._go("core", [(here, here)])

    def finish(self, step):
        for m in self.wait_for:
            m.wait_recv()
        if step == 0:
            if self.ready is not None:
                self.ready()

            @pl.loop(0, 1024 // 64)
            def _(i):
                r = pl.ds(pl.multiple_of(i * 64, 64), 64)
                self.acc[r, self.cols] = self.acc[r, self.cols] + self.inbox_core[r, self.cols]
        elif step <= 6:
            for at, box, count in self.adds:
                chunk = min(count, 64)

                @pl.loop(0, count // chunk)
                def _(i):
                    r = pl.ds(pl.multiple_of(at + i * chunk, 16), chunk)
                    q = pl.ds(pl.multiple_of(box + i * chunk, 16), chunk)
                    self.acc[r, self.cols] = self.acc[r, self.cols] + self.inbox[q, self.cols]
            if step == 6:
                self.gat[pl.ds(pl.multiple_of(self.off, 16), self.span), self.mine] = self.acc[
                    rows(self.y, self.off, self.span), self.cols]
        elif step <= 10:
            self.off = self.off - self.me.bit(self.back[step - 7]) * self.span
            self.span *= 2

    def close(self):
        for m in self.sent:
            m.wait_send()


class Timeline:
    def __init__(self):
        self.now, self.free, self.queue, self.count, self.parts = 0.0, {}, [], 0, []

    def launch(self, part, step=0):
        if step == 0:
            self.parts.append(part)
            part.over, part.past = False, -1
        link, size, cost = part.load(step)
        part.start(step)
        begin = max(self.now, self.free.get(link, 0.0))
        end = begin + size / (0.45e6 if link == "core" else 0.036e6)
        self.free[link] = end
        heapq.heappush(self.queue, (end + (1.5 if link == "core" else 3.0), self.count, part, step, cost))
        self.count += 1

    def _one(self):
        end, _, part, step, cost = heapq.heappop(self.queue)
        self.now = max(self.now, end)
        part.finish(step)
        part.over, part.past = step + 1 == part.steps, step
        self.now += cost
        if step + 1 < part.steps:
            self.launch(part, step + 1)

    def poll(self):
        while self.queue and self.queue[0][0] <= self.now:
            self._one()

    def work(self, what, time):
        what()
        self.now += time
        self.poll()

    def until(self, parts, step=9):
        while any(not p.over and p.past < step for p in parts):
            self._one()

    def drain(self):
        while self.queue:
            self._one()
        for part in self.parts:
            part.close()


def rotated(i):
    return tuple(LINKS[(i + j) % 6] for j in range(6))


def reduce_parts(me, sems, terms, acc, inbox, inbox_core, gat, ready):
    columns = terms.shape[1]
    half = columns // 2
    n, starts = (6, (0, 1, 2, 3, 4, 5)) if columns == 3072 else (4, (0, 1, 3, 4))
    width = half // n
    out = []
    for i in range(n):
        source = terms.at[:, pl.ds(pl.multiple_of((1 - me.c) * half + i * width, 128), width)]
        out.append(Reduce(me, sems, source, acc, inbox, inbox_core, gat, width, i * width, me.c * half + i * width,
                          rotated(starts[i]), ready if i == 0 else None))
    return out


def gather_parts(me, sems, shard, full):
    half = full.shape[1] // 2
    width = half // 4
    orders = (("yA", "yB", "xA", "xB"), ("yB", "yA", "zA", "zB"), ("yA", "yB", "xB", "xA"), ("yB", "yA", "zB", "zA"))
    return [Gather(me, sems, shard, full, width, me.c * half + i * width, order) for i, order in enumerate(orders)]


FAR = -1e30


def heads_apart(block):
    first = lax.broadcasted_iota(jnp.int32, block.shape, 1) < 64
    zero = jnp.zeros_like(block)
    return jnp.concatenate([jnp.where(first, block, zero), jnp.where(first, zero, block)], axis=0)


def heads_together(wide):
    count = wide.shape[1] // 2
    return jnp.concatenate([wide[:64, :count], wide[64:, count:]], axis=0).T


def nt(a, b):
    return lax.dot_general(a, b, (((1,), (1,)), ((), ())), preferred_element_type=jnp.float32)


def tn(a, b):
    return lax.dot_general(a, b, (((0,), (0,)), ((), ())), preferred_element_type=jnp.float32)


def nn(a, b):
    return jnp.dot(a, b, preferred_element_type=jnp.float32)


def window_bias(key_span, query_span, low, high):
    gap = key_span - query_span
    return jnp.where((gap >= low) & (gap <= high), 0.0, FAR).astype(jnp.float32)


def prob_of(keys, queries, bias):
    score = nt(keys, queries) + jnp.concatenate([bias, bias], axis=1)
    terms = jnp.exp(score - jnp.max(score, axis=0, keepdims=True))
    return terms * (1.0 / jnp.sum(terms, axis=0, keepdims=True))


class Spans:
    def __init__(self, me, length, size):
        self.first, self.length = me.seq * 384, length[0]
        self.inverse = 1.0 / jnp.full((1, 1), size[0].astype(jnp.float32))

    def at(self, start, count, axis):
        shape = (count, 1) if axis == 0 else (1, count)
        return self.first + start + lax.broadcasted_iota(jnp.int32, shape, axis)

    def number(self, frames):
        return jnp.floor((frames.astype(jnp.float32) + 0.5) * self.inverse)

    def bias(self, query, key, count, low, high):
        frames = self.at(key, count, 0)
        alive = (frames >= 0) & (frames < self.length)
        return window_bias(jnp.where(alive, self.number(frames), 1e6), self.number(self.at(query, 128, 1)), low, high)


UP_BLOCKS = ((0, 0, 256), (128, 64, 320), (256, 192, 320))
DIT_BLOCKS = ((0, 0, 384), (128, 128, 384), (256, 256, 320))


def first_kernel(x0, cot, s0, s1, s2, s3, length, size,
                 act1, halo1, n0t, inv0, n1t, dact, mix1, mix2, result, dh, dmix1, w1_out,
                 w1, p1, w2, p2, n0, n1, inv1, hidden, act2, halo2, dmix2, dn, sums, hout, hin, bias1, bias2, live, send, recv, local):
    me = Place()
    spans = Spans(me, length, size)
    bf, f32 = jnp.bfloat16, jnp.float32
    sems = Sems(send, recv)
    shards, fulls = (s0, s1, s2, s3), (w1, p1, w2, p2)
    own = [pltpu.make_async_copy(s, f.at[rows(me.y, 0, 256), :], local.at[i]) for i, (s, f) in enumerate(zip(shards, fulls, strict=True))]
    for cp in own:
        cp.start()
    greet(me, "next", "previous")
    line = Timeline()
    parts = [gather_parts(me, sems, s, f) for s, f in zip(shards, fulls, strict=True)]

    def fetch(i):
        for part in parts[i]:
            line.launch(part)

    def have(i):
        line.until(parts[i])
        own[i].wait()

    def chunks(count, width):
        def run(body):
            @pl.loop(0, count)
            def _(i):
                body(pl.ds(pl.multiple_of(i * width, width), width))
        return run

    def normalize(source, normed, inverse):
        @chunks(6, 64)
        def _(r):
            value, inv = normalize_rows(source[r, :].astype(f32))
            normed[r, :] = value.astype(bf)
            inverse[r, :] = inv

    def turn(normed, turned):
        @chunks(4, 256)
        def _(c):
            turned[c, :] = normed[:, c].T

    def project(normed, weight, act, low, high):
        @pl.loop(low, high)
        def _(i):
            c = pl.ds(pl.multiple_of(i * 512, 512), 512)
            act[:, c] = nn(normed[...], weight[:, c]).astype(bf)

    def heads(k, body):
        @pl.loop(2 * k, 2 * k + 2)
        def _(g):
            at = pl.multiple_of(g * 128, 128)
            body(pl.ds(at, 128), pl.ds(at + 1024, 128), pl.ds(at + 2048, 128))

    def up_block(i, q_at, k_at, v_at):
        r0, k0, n = UP_BLOCKS[i]
        keys, values = act1[k0:min(k0 + n, 384), k_at], act1[k0:min(k0 + n, 384), v_at]
        if i == 2:
            keys = jnp.concatenate([keys, halo1[:, q_at]], axis=0)
            values = jnp.concatenate([values, halo1[:, k_at]], axis=0)
        queries = heads_apart(act1[r0:r0 + 128, q_at] * jnp.bfloat16(0.125))
        p = prob_of(keys, queries, bias1[i, :n])
        mix1[r0:r0 + 128, q_at] = (heads_together(tn(values, p.astype(bf))) * live[r0:r0 + 128]).astype(bf)

    def up_early(k):
        def body(*at):
            up_block(0, *at)
            up_block(1, *at)
        heads(k, body)

    def up_late(k):
        heads(k, lambda *at: up_block(2, *at))

    def dit_block(i, q_at, k_at, v_at):
        r0, k0, n = DIT_BLOCKS[i]
        keys, values = act2[max(k0 - 192, 0):k0 - 192 + n, k_at], act2[max(k0 - 192, 0):k0 - 192 + n, v_at]
        if k0 < 192:
            keys = jnp.concatenate([halo2[k0:, q_at], keys], axis=0)
            values = jnp.concatenate([halo2[k0:, k_at], values], axis=0)
        queries = heads_apart(act2[r0:r0 + 128, q_at] * jnp.bfloat16(0.125))
        p = prob_of(keys, queries, bias2[i, :n])
        low = p.astype(bf)
        mix2[r0:r0 + 128, q_at] = (heads_together(tn(values, low)) * live[r0:r0 + 128]).astype(bf)
        dout = heads_apart(dmix2[r0:r0 + 128, q_at])
        dp = nt(values, dout)
        ds = (p * (dp - jnp.sum(p * dp, axis=0, keepdims=True))).astype(bf)
        dact[r0:r0 + 128, q_at] = (heads_together(tn(keys, ds)) * 0.125).astype(bf)
        return nn(ds, queries), nn(low, dout)

    def dit_early(k):
        def body(q_at, k_at, v_at):
            dk, dv = dit_block(2, q_at, k_at, v_at)
            for at, d in ((q_at, dk), (k_at, dv)):
                sums[:256, at] = jnp.zeros((256, 128), f32)
                sums[256:, at] = d
        heads(k, body)

    flights = {}

    def dit_late(k):
        def body(q_at, k_at, v_at):
            for i in (0, 1):
                _, k0, n = DIT_BLOCKS[i]
                dk, dv = dit_block(i, q_at, k_at, v_at)
                sums[k0:k0 + n, q_at] += dk
                sums[k0:k0 + n, k_at] += dv
            for at, to in ((q_at, k_at), (k_at, v_at)):
                hout[:, at] = sums[:192, at].astype(bf)
                dact[:192, to] = sums[192:384, at].astype(bf)
        heads(k, body)
        flights[k] = [sems.copy(me, "previous", hout.at[:, c], hin.at[:, c]) for c in (pl.ds(256 * k, 256), pl.ds(1024 + 256 * k, 256))]
        for m in flights[k]:
            m.start()

    def settle(k):
        for m in flights[k]:
            m.wait_recv()
        for first in (256 * k, 1024 + 256 * k):
            c = pl.ds(first, 256)
            dact[192:, pl.ds(1024 + first, 256)] = (sums[384:, c] + hin[:, c].astype(f32)).astype(bf)

    def mixed_back(grad, weight, out):
        @chunks(4, 256)
        def _(c):
            out[:, c] = (nt(grad[...], weight[c, :]) * live[...]).astype(bf)

    def add_mixed(base, mix, weight, out):
        @chunks(4, 256)
        def _(c):
            out[:, c] = (base[:, c].astype(f32) + nn(mix[...], weight[:, c])).astype(bf)

    def normed_back():
        @chunks(4, 256)
        def _(c):
            dn[:, c] = nt(dact[...], w2[c, :])

    def hidden_back():
        @chunks(6, 64)
        def _(r):
            dh[r, :] = (cot[r, :].astype(f32) + norm_backward(hidden[r, :].astype(f32), inv1[r, :], dn[r, :])).astype(bf)

    def biases():
        for i, (r0, k0, n) in enumerate(UP_BLOCKS):
            bias1[i, :n] = spans.bias(r0, k0, n, 0, 1)
        for i, (r0, k0, n) in enumerate(DIT_BLOCKS):
            bias2[i, :n] = spans.bias(r0, k0 - 192, n, -2, 0)
        live[...] = (spans.at(0, 384, 0) < spans.length).astype(f32)

    fetch(0)
    line.work(lambda: normalize(x0, n0, inv0), 1.5)
    line.work(biases, 0.7)
    line.work(lambda: turn(n0, n0t), 0.8)
    line.until(parts[0], 1)
    fetch(1)
    fetch(2)
    have(0)
    fetch(3)
    keep = pltpu.make_async_copy(w1, w1_out, local.at[4])
    keep.start()
    line.work(lambda: project(n0, w1, act1, 2, 6), 2.0)
    give1 = sems.copy(me, "previous", act1.at[pl.ds(0, 128), pl.ds(1024, 2048)], halo1)
    give1.start()
    line.work(lambda: project(n0, w1, act1, 0, 2), 1.0)
    for k in range(4):
        line.work(lambda: up_early(k), 1.5)
    give1.wait_recv()
    for k in range(4):
        line.work(lambda: up_late(k), 0.9)
    have(1)
    line.work(lambda: add_mixed(x0, mix1, p1, hidden), 1.0)
    line.work(lambda: normalize(hidden, n1, inv1), 1.2)
    have(2)
    line.work(lambda: project(n1, w2, act2, 2, 6), 2.0)
    give2 = sems.copy(me, "next", act2.at[pl.ds(192, 192), pl.ds(1024, 2048)], halo2)
    give2.start()
    line.work(lambda: project(n1, w2, act2, 0, 2), 1.0)
    have(3)
    line.work(lambda: mixed_back(cot, p2, dmix2), 1.0)
    line.drain()
    for k in range(4):
        dit_early(k)
    turn(n1, n1t)
    give2.wait_recv()
    for k in range(4):
        dit_late(k)
        if k:
            settle(k - 1)
    add_mixed(hidden, mix2, p2, result)
    settle(3)
    normed_back()
    hidden_back()
    mixed_back(dh, p1, dmix1)
    keep.wait()
    for m in [give1, give2] + [m for made in flights.values() for m in made]:
        m.wait_send()


def first_part(*args):
    bf, f32 = jnp.bfloat16, jnp.float32
    v, h = pl.BlockSpec(memory_space=pltpu.VMEM), pl.BlockSpec(memory_space=pl.ANY)
    s = lambda shape, dt=bf: pltpu.VMEM(shape, dt)
    o = lambda *shape, dt=bf: jax.ShapeDtypeStruct(shape, dt)
    scratch = [s((1024, 3072)), s((1024, 1024)), s((1024, 3072)), s((1024, 1024)), s((384, 1024)), s((384, 1024)), s((384, 1), f32),
               s((384, 1024)), s((384, 3072)), s((192, 2048)), s((384, 1024)), s((384, 1024), f32), s((576, 2048), f32),
               s((192, 2048)), s((192, 2048)), s((3, 384, 128), f32), s((3, 384, 128), f32), s((384, 1), f32),
               pltpu.SemaphoreType.DMA((400,)), pltpu.SemaphoreType.DMA((400,)), pltpu.SemaphoreType.DMA((5,))]
    return pl.pallas_call(
        first_kernel,
        out_shape=[o(384, 3072), o(128, 2048), o(1024, 384), o(384, 1, dt=f32), o(1024, 384), o(384, 3072)] + [o(384, 1024)] * 5 + [o(1024, 3072)],
        in_specs=[v] * 2 + [h] * 4 + [pl.BlockSpec(memory_space=pltpu.SMEM)] * 2, out_specs=[v] * 11 + [h], scratch_shapes=scratch,
        compiler_params=pltpu.CompilerParams(collective_id=1, has_side_effects=True, vmem_limit_bytes=60 << 20),
        name="first_part",
    )(*args)


def last_kernel(gp2, gw2, gp1, act, halo, dm, dh_far, x0_far, inv, n0t, w1_far, length, size,
                dframes, t1, tp1, t2, tp2,
                acc1, accp1, acc2, accp2, in1, inp1, in2, inp2, co1, cop1, co2, cop2,
                outbox, kx, vx, bias, dkx, dvx, edge, hout, hin, dact, dcat, dn, dh, x0, w1, send, recv, local):
    me = Place()
    spans = Spans(me, length, size)
    bf = jnp.bfloat16
    sems = Sems(send, recv)
    loads = []
    for i, (t, acc) in enumerate(((gp2, accp2), (gw2, acc2), (gp1, accp1))):
        half = t.shape[1] // 2
        cp = pltpu.make_async_copy(t.at[:, pl.ds(pl.multiple_of(me.c * half, 128), half)], acc, local.at[i])
        cp.start()
        loads.append(cp)
    late = [pltpu.make_async_copy(far, near, local.at[3 + i]) for i, (far, near) in enumerate(((w1_far, w1), (dh_far, dh), (x0_far, x0)))]
    for cp in late:
        cp.start()
    for i, (r0, k0, n) in enumerate(UP_BLOCKS):
        bias[i, :n] = spans.bias(r0, k0, n, 0, 1)
    greet(me, "next", "previous")
    line = Timeline()
    for i, (t, acc, box, core, gat) in enumerate(((gp2, accp2, inp2, cop2, tp2), (gw2, acc2, in2, co2, t2), (gp1, accp1, inp1, cop1, tp1))):
        for part in reduce_parts(me, sems, t, acc, box, core, gat, loads[i].wait):
            line.launch(part)

    flights = {}

    def attend(g0):
        @pl.loop(g0, g0 + 1)
        def _(g):
            at = pl.multiple_of(g * 128, 128)
            q_at, k_at, v_at = pl.ds(at, 128), pl.ds(at + 1024, 128), pl.ds(at + 2048, 128)
            kx[:384], kx[384:] = act[:, k_at], halo[:, q_at]
            vx[:384], vx[384:] = act[:, v_at], halo[:, k_at]
            dkx[...] = jnp.zeros_like(dkx)
            dvx[...] = jnp.zeros_like(dvx)
            for i, (r0, k0, n) in enumerate(UP_BLOCKS):
                keys, values = kx[k0:k0 + n], vx[k0:k0 + n]
                queries = heads_apart(act[r0:r0 + 128, q_at] * jnp.bfloat16(0.125))
                p = prob_of(keys, queries, bias[i, :n])
                dout = heads_apart(dm[r0:r0 + 128, q_at])
                dp = nt(values, dout)
                ds = (p * (dp - jnp.sum(p * dp, axis=0, keepdims=True))).astype(bf)
                dvx[k0:k0 + n] += nn(p.astype(bf), dout)
                dkx[k0:k0 + n] += nn(ds, queries)
                dact[r0:r0 + 128, q_at] = (heads_together(tn(keys, ds)) * 0.125).astype(bf)
            for full, c_at, e_at in ((dkx, k_at, q_at), (dvx, v_at, k_at)):
                edge[:, e_at] = full[:128]
                dact[128:, c_at] = full[128:384].astype(bf)
                hout[:, e_at] = full[384:].astype(bf)

        if g0 % 2 == 0:
            return
        k = g0 // 2
        made = []
        for first in (0, 1024):
            c = pl.ds(first + 256 * k, 256)
            made.append(sems.copy(me, "next", hout.at[:, c], hin.at[:, c]))
        for m in made:
            m.start()
        flights[k] = made

    def settle(k):
        for m in flights[k]:
            m.wait_recv()
        for first in (0, 1024):
            c = pl.ds(first + 256 * k, 256)
            dact[:128, pl.ds(1024 + first + 256 * k, 256)] = (edge[:, c] + hin[:, c].astype(jnp.float32)).astype(bf)
        for which in range(3):
            mine = pl.ds(pl.multiple_of(which * 1024 + (2 * k + me.c) * 128, 128), 128)
            his = pl.ds(pl.multiple_of(which * 1024 + (2 * k + 1 - me.c) * 128, 128), 128)
            dcat[:, which * 128:which * 128 + 128] = dact[:, mine]
            dcat[:, 384 + which * 128:512 + which * 128] = dact[:, his]

        @pl.loop(0, 4)
        def _(i):
            r = pl.ds(pl.multiple_of(i * 256, 256), 256)
            t = nn(n0t[r, :], dcat[...]).astype(bf)
            acc1[r, k * 384:k * 384 + 384] = t[:, :384]
            outbox[r, k * 384:k * 384 + 384] = t[:, 384:]

    def send_terms(k):
        for which in range(3):
            at = k * 384 + which * 128
            line.launch(Reduce(me, sems, outbox.at[:, pl.ds(at, 128)], acc1, in1, co1, t1, 128, at,
                               which * 1024 + (2 * k + me.c) * 128, rotated(which + 3 * (k % 2))))

    def back_to_normed(i0):
        @pl.loop(i0, i0 + 1)
        def _(i):
            r = pl.ds(pl.multiple_of(i * 256, 256), 256)
            dn[:, r] = nt(dact[...], w1[r, :])

    def back_to_frames():
        @pl.loop(0, 6)
        def _(i):
            r = pl.ds(pl.multiple_of(i * 64, 64), 64)
            x = x0[r, :].astype(jnp.float32)
            inverse = inv[r, :]
            dframes[r, :] = (dh[r, :].astype(jnp.float32) + norm_backward(x, inverse, dn[r, :])).astype(bf)

    line.work(lambda: attend(0), 2.0)
    line.work(lambda: attend(1), 2.0)
    for k in range(1, 4):
        line.work(lambda: attend(2 * k), 2.0)
        line.work(lambda: attend(2 * k + 1), 2.0)
        line.work(lambda: settle(k - 1), 1.2)
        send_terms(k - 1)
    line.work(lambda: settle(3), 1.2)
    send_terms(3)
    for cp in late:
        cp.wait()
    for i in range(4):
        line.work(lambda: back_to_normed(i), 1.0)
    line.work(back_to_frames, 1.0)
    line.drain()
    for made in flights.values():
        for m in made:
            m.wait_send()


def last_part(*args):
    bf, f32 = jnp.bfloat16, jnp.float32
    v, h = pl.BlockSpec(memory_space=pltpu.VMEM), pl.BlockSpec(memory_space=pl.ANY)
    s = lambda shape, dt=bf: pltpu.VMEM(shape, dt)
    sizes = (3072, 1024, 3072, 1024)
    scratch = [s((1024, c // 2)) for _ in range(3) for c in sizes]
    scratch += [s((1024, 1536)), s((512, 128)), s((512, 128)), s((3, 384, 128), f32), s((512, 128), f32), s((512, 128), f32),
                s((128, 2048), f32), s((128, 2048)), s((128, 2048)), s((384, 3072)), s((384, 768)), s((384, 1024), f32),
                s((384, 1024)), s((384, 1024)), s((1024, 3072)),
                pltpu.SemaphoreType.DMA((520,)), pltpu.SemaphoreType.DMA((520,)), pltpu.SemaphoreType.DMA((6,))]
    return pl.pallas_call(
        last_kernel,
        out_shape=[jax.ShapeDtypeStruct((384, 1024), bf)] + [jax.ShapeDtypeStruct((256, c), bf) for c in sizes],
        in_specs=[h] * 3 + [v] * 3 + [h] * 2 + [v] * 2 + [h] + [pl.BlockSpec(memory_space=pltpu.SMEM)] * 2, out_specs=[v] * 5, scratch_shapes=scratch,
        compiler_params=pltpu.CompilerParams(collective_id=2, has_side_effects=True, vmem_limit_bytes=60 << 20),
        name="last_part",
    )(*args)


EPS = 1e-06
DEAD = 1 << 20


def normalize_rows(xfull):
    inverse = lax.rsqrt(jnp.mean(xfull * xfull, axis=-1, keepdims=True) + EPS)
    return (xfull * inverse, inverse)


def norm_backward(xfull, inverse, d_normed):
    row_inner = jnp.mean(d_normed * xfull, axis=-1, keepdims=True)
    return inverse * d_normed - xfull * (inverse * inverse * inverse) * row_inner


def term(left, right):
    return lax.dot_general(left, right, (((0,), (0,)), ((), ())), preferred_element_type=jnp.float32).astype(jnp.bfloat16)


def local(frames, valid_length, span_frames, w1_shard, p1_shard, w2_shard, p2_shard, cotangent):
    bf, f32 = jnp.bfloat16, jnp.float32
    x0, cot = frames[0], cotangent[0]
    act1, halo1, n0t, inv0, n1t, dact2, mix1, mix2, result, dhidden, dmix1, w1 = first_part(
        x0, cot, w1_shard, p1_shard, w2_shard, p2_shard, valid_length, span_frames)
    gp2 = term(mix2, cot)
    gw2 = nn(n1t, dact2).astype(bf)
    gp1 = term(mix1, dhidden)
    scale = float(8 * 6144) ** -0.5
    dframes, *totals = last_part(gp2, gw2, gp1, act1, halo1, dmix1, dhidden, x0, inv0, n0t, w1, valid_length, span_frames)
    return (result[None], dframes[None], *(t.astype(f32) * scale for t in totals))


def solution(mesh):
    rows3, row, flat = P(("fsdp", "dp"), "seq", None), P("fsdp", None), P(("fsdp", "dp"))
    return jax.shard_map(
        local, mesh=mesh, in_specs=(rows3, flat, flat, row, row, row, row, rows3),
        out_specs=(rows3, rows3, row, row, row, row), check_vma=False)
```
